32 devices in a mesh: client: 8 (over y, x, core), unit: 4 (over z).
Axes of the slice: x: 2, y: 2, z: 4, core: 2. Of those that a mesh axis runs over, the one named last changes fastest.
Arguments:
- token_ids: int32 [256], replicated, may hold values from 0 to 65535
- embed_table: bfloat16 [65536, 4096], P(('client', 'unit')), may hold values from -6 to 6
- norm_gain: float32 [4096], replicated, may hold values from 0.5 to 1.5
- client_gate: bfloat16 [8, 4096, 7168], P('client', None, 'unit'), may hold values from -0.09375 to 0.09375
- client_up: bfloat16 [8, 4096, 7168], P('client', None, 'unit'), may hold values from -0.09375 to 0.09375
- ref_gate: bfloat16 [4096, 7168], P('client', 'unit'), may hold values from -0.09375 to 0.09375
- ref_up: bfloat16 [4096, 7168], P('client', 'unit'), may hold values from -0.09375 to 0.09375
Outputs:
- merged: float32 [7168, 256], P('unit')
- score: float32 [8, 7168], P('client', 'unit')
The draws below stay inside these ranges and needn't reach their ends.
All inputs are finite; a program needn't handle non-finite values.
Results may differ from the reference program's by a relative error of at most 0.014.
Values may be sent and summed in bfloat16 or wider, within the bound.
No kernel may reach another device: no remote copies, remote signals or barrier semaphores. Data moves between devices by JAX's collectives and lax.ppermute only.
A program may use at most 128 MiB of HBM per device.

```python
import math
import jax
import jax.numpy as jnp
import numpy as np
from jax import lax

D = 4096
FF = 7168
VOCAB = 65536
TOKENS = 256
CLIENTS = 8


def plant(values, stream_key, smallest, largest):
    longest = values.shape.index(max(values.shape))
    spots = []
    for shift in (0, 1):
        where = [jax.random.randint(jax.random.fold_in(stream_key, axis), (), 0, length) for axis, length in enumerate(values.shape)]
        where[longest] = (where[longest] + shift) % values.shape[longest]
        spots.append(tuple(where))
    return values.at[spots[0]].set(smallest).at[spots[1]].set(largest)


def shard_levels(key, dims, pieces, least, top_value):
    def one(position, shards_of):
        draws = jax.random.uniform(jax.random.fold_in(jax.random.fold_in(key, 6), position), (shards_of,), jnp.float32, least / len(pieces), top_value / len(pieces))
        return jnp.repeat(jnp.exp(draws), dims[position] // shards_of).reshape((-1,) + (1,) * (len(dims) - position - 1))

    factor_of = one(*pieces[0])
    for cut in pieces[1:]:
        factor_of = factor_of * one(*cut)
    return factor_of


def rank_table(number_of, slope):
    loads = [(1 << 20) // math.isqrt(grade ** slope) + 1 for grade in range(1, number_of + 1)]
    scale = 1 + sum(loads) // (1 << 30)
    return np.cumsum(np.array([max(1, weight // scale) for weight in loads]))


def ranked(stream_key, shape, amount, slope):
    listing = rank_table(amount, slope)
    lot = jax.random.randint(jax.random.fold_in(stream_key, 1), shape, 0, int(listing[amount - 1]))
    rank = jnp.searchsorted(jnp.asarray(listing, jnp.int32), lot, side="right")
    return jax.random.permutation(jax.random.fold_in(stream_key, 2), amount)[rank].astype(jnp.int32)


def normal_values(key, extent, width, bound, split=(), kind=jnp.bfloat16):
    entries = jax.random.normal(key, extent, jnp.float32) * width
    if len(split) > 0:
        entries = shard_levels(key, extent, split, -0.22, 0.18) * entries
    return jnp.clip(entries, min=-bound, max=bound).astype(kind)


def setup_inputs(seed: int = 0) -> dict:
    arg_keys = jax.random.split(jax.random.key(seed), 8)
    token_ids = plant(ranked(arg_keys[0], (TOKENS,), VOCAB, 2), jax.random.fold_in(arg_keys[0], 3), 0, VOCAB - 1).astype(jnp.int32)
    embed_table = normal_values(arg_keys[1], (VOCAB, D), 1.0, 6.0, ((0, 32),))
    norm_gain = jnp.clip(1.0 + 0.1 * jax.random.normal(arg_keys[2], (D,), jnp.float32), 0.5, 1.5)
    client_gate = normal_values(arg_keys[3], (CLIENTS, D, FF), D ** -0.5, 0.09375, ((0, 8), (2, 4)))
    client_up = normal_values(arg_keys[4], (CLIENTS, D, FF), D ** -0.5, 0.09375, ((0, 8), (2, 4)))
    ref_gate = normal_values(arg_keys[5], (D, FF), D ** -0.5, 0.09375, ((0, 8), (1, 4)))
    ref_up = normal_values(arg_keys[6], (D, FF), D ** -0.5, 0.09375, ((0, 8), (1, 4)))
    return {"token_ids": token_ids, "embed_table": embed_table, "norm_gain": norm_gain, "client_gate": client_gate, "client_up": client_up, "ref_gate": ref_gate, "ref_up": ref_up}


sharpness = 40.0

def standardize(hidden):
    center = lax.optimization_barrier(jnp.mean(hidden, axis=0, keepdims=True))
    shifted = hidden - center
    spread = jnp.sqrt(lax.optimization_barrier(jnp.mean(shifted * shifted, axis=0, keepdims=True)) + 1e-06)
    return (shifted / spread).astype(jnp.bfloat16)

def activate(normed, gate_weight, up_weight):
    gate = jnp.dot(normed, gate_weight, preferred_element_type=jnp.float32)
    up = jnp.dot(normed, up_weight, preferred_element_type=jnp.float32)
    return standardize(jax.nn.silu(gate) * up)

def reference(token_ids, embed_table, norm_gain, client_gate, client_up, ref_gate, ref_up):
    rows = jnp.take(embed_table, token_ids, axis=0).astype(jnp.float32)
    scale = lax.rsqrt(lax.optimization_barrier(jnp.mean(rows * rows, axis=1, keepdims=True)) + 1e-05)
    normed = (rows * scale * norm_gain[None, :]).astype(jnp.bfloat16)
    ref_std = activate(normed, ref_gate, ref_up)

    def per_client(total, pair):
        gate_weight, up_weight = pair
        client_std = activate(normed, gate_weight, up_weight)
        correlation = jnp.dot(client_std.T, ref_std, preferred_element_type=jnp.float32) * (1.0 / TOKENS)
        weights = jnp.exp(sharpness * correlation)
        colsum = lax.optimization_barrier(jnp.sum(weights, axis=0))
        weighted = lax.optimization_barrier(jnp.sum(weights * correlation, axis=0))
        numerator = lax.dot_general(weights.astype(jnp.bfloat16), client_std, (((0,), (1,)), ((), ())), preferred_element_type=jnp.float32)
        matched = numerator / colsum[:, None]
        return (total + matched, weighted / colsum)
    start_total = jnp.zeros((FF, TOKENS), jnp.float32)
    total, score = lax.scan(per_client, start_total, (client_gate, client_up))
    return (total / CLIENTS, score)
```

```python
import functools

import jax
import jax.numpy as jnp
from jax import lax
from jax.experimental import pallas as pl
from jax.experimental.pallas import tpu as pltpu
from jax.sharding import PartitionSpec as P

sharpness = 40.0
log2_e = 1.4426950408889634
group_rows = 16
fetch_slots = 16
bf16 = jnp.bfloat16
f32 = jnp.float32
whole = pl.BlockSpec(memory_space=pltpu.VMEM)
scalars = pl.BlockSpec(memory_space=pltpu.SMEM)
anywhere = pl.BlockSpec(memory_space=pl.ANY)


def vmem_params(mib):
    return pltpu.CompilerParams(vmem_limit_bytes=mib * 1024 * 1024)


def cost(flops, bytes_accessed, transcendentals=0):
    return pl.CostEstimate(
        flops=int(flops), bytes_accessed=int(bytes_accessed), transcendentals=int(transcendentals)
    )


def xor_permute(value, axis, size, mask):
    return lax.ppermute(value, axis, [(i, i ^ mask) for i in range(size)])


def select_kernel(ids, place, gain, table, keep, send, rows, held, slots, sems):
    tokens, width = rows.shape
    rows_here = table.shape[0]
    start = place[0] * rows_here
    client = place[1]

    def note(t, count):
        local = ids[t] - start
        mine = jnp.logical_and(local >= 0, local < rows_here)

        @pl.when(mine)
        def _():
            held[count] = t

        return count + jnp.where(mine, 1, 0)

    def fetch(k):
        t = held[k]
        group = pl.multiple_of((ids[t] - start) // group_rows * group_rows, group_rows)
        slot = lax.rem(k, fetch_slots)
        return pltpu.make_async_copy(
            table.at[pl.ds(group, group_rows), :], slots.at[slot], sems.at[slot]
        )

    count = lax.fori_loop(0, tokens, note, jnp.int32(0))

    def begin(k, carry):
        fetch(k).start()
        return carry

    lax.fori_loop(0, jnp.minimum(count, fetch_slots), begin, 0)
    rows[...] = jnp.zeros_like(rows)
    sublane = lax.broadcasted_iota(jnp.int32, (group_rows, width), 0)

    def place_row(k, carry):
        fetch(k).wait()
        t = held[k]
        row_in_group = lax.rem(ids[t] - start, group_rows)
        block = slots[lax.rem(k, fetch_slots)].astype(f32)
        row = jnp.sum(jnp.where(sublane == row_in_group, block, 0.0), axis=0, keepdims=True)
        scale = lax.rsqrt(jnp.sum(row * row, axis=1, keepdims=True) * (1.0 / width) + 1e-05)
        rows[pl.ds(t, 1), :] = row * scale * gain[...]

        @pl.when(k + fetch_slots < count)
        def _():
            fetch(k + fetch_slots).start()

        return carry

    lax.fori_loop(0, count, place_row, 0)
    span = keep.shape[2]
    for p in range(2 * keep.shape[0]):
        source = pl.multiple_of((client ^ p) * span, span)
        target = send if p % 2 else keep
        target[p // 2] = rows[:, pl.ds(source, span)].astype(bf16)


def select_rows(token_ids, place, norm_gain, embed_table, clients):
    tokens, width = token_ids.shape[0], embed_table.shape[1]
    half = jax.ShapeDtypeStruct((clients // 2, tokens, width // clients), bf16)
    return pl.pallas_call(
        select_kernel,
        out_shape=(half, half),
        in_specs=[scalars, scalars, whole, anywhere],
        out_specs=(whole, whole),
        scratch_shapes=[
            pltpu.VMEM((tokens, width), f32),
            pltpu.SMEM((tokens,), jnp.int32),
            pltpu.VMEM((fetch_slots, group_rows, width), bf16),
            pltpu.SemaphoreType.DMA((fetch_slots,)),
        ],
        compiler_params=vmem_params(24),
        cost_estimate=cost(4e6, 4e6),
        name="select_rows",
    )(token_ids, place, norm_gain[None, :], embed_table)


def standardized(hidden, axis):
    count = hidden.shape[axis]
    center = jnp.sum(hidden, axis=axis, keepdims=True) * (1.0 / count)
    shifted = hidden - center
    spread = jnp.sum(shifted * shifted, axis=axis, keepdims=True) * (1.0 / count)
    return (shifted * lax.rsqrt(spread + 1e-06)).astype(bf16)


def gated(gate, up):
    return gate / (1.0 + jnp.exp(-gate)) * up


def client_kernel(place, *refs):
    *blocks, gate_w, up_w, out = refs
    client = place[1]
    span = blocks[0].shape[1]
    gate = jnp.zeros(out.shape, f32)
    up = jnp.zeros(out.shape, f32)
    for p, block in enumerate(blocks):
        at = pl.ds(pl.multiple_of((client ^ p) * span, span), span)
        gate += jnp.dot(block[...], gate_w[0, at, :], preferred_element_type=f32)
        up += jnp.dot(block[...], up_w[0, at, :], preferred_element_type=f32)
    out[...] = standardized(gated(gate, up), 0)


def unit_block(units, most=256):
    return most if units % most == 0 else most // 2


def client_activations(place, blocks, client_gate, client_up):
    tokens, span = blocks[0].shape
    _, width, units = client_gate.shape
    wide = unit_block(units)
    weights = pl.BlockSpec((1, width, wide), lambda i: (0, 0, i))
    return pl.pallas_call(
        client_kernel,
        grid=(units // wide,),
        out_shape=jax.ShapeDtypeStruct((tokens, units), bf16),
        in_specs=[scalars]
        + [pl.BlockSpec((tokens, span), lambda i: (0, 0))] * len(blocks)
        + [weights, weights],
        out_specs=pl.BlockSpec((tokens, wide), lambda i: (0, i)),
        compiler_params=vmem_params(40),
        cost_estimate=cost(4 * tokens * width * units, 4 * width * units),
        name="client_activations",
    )(place, *blocks, client_gate, client_up)


def partial_kernel(place, rows, gate_w, up_w, keep, send, total):
    step = pl.program_id(0)
    wide = gate_w.shape[1]
    at = pl.ds(pl.multiple_of(step * wide, wide), wide)
    total[0, at, :] = jnp.dot(rows[...], gate_w[...], preferred_element_type=f32).T
    total[1, at, :] = jnp.dot(rows[...], up_w[...], preferred_element_type=f32).T

    @pl.when(step == pl.num_programs(0) - 1)
    def _():
        piece = keep.shape[2]
        for p in range(2 * keep.shape[0]):
            source = pl.ds(pl.multiple_of((place[1] ^ p) * piece, 8), piece)
            for which in range(2):
                if p % 2:
                    send[p // 2, which] = total[which, source, :].astype(bf16)
                else:
                    keep[p // 2, which] = total[which, source, :]


def reference_partials(place, rows, ref_gate, ref_up, clients):
    tokens, span = rows.shape
    units = ref_gate.shape[1]
    wide = unit_block(units)
    shape = (clients // 2, 2, units // clients, tokens)
    weights = pl.BlockSpec((span, wide), lambda i: (0, i))
    pieces = pl.BlockSpec(shape, lambda i: (0, 0, 0, 0))
    return pl.pallas_call(
        partial_kernel,
        grid=(units // wide,),
        out_shape=(jax.ShapeDtypeStruct(shape, f32), jax.ShapeDtypeStruct(shape, bf16)),
        in_specs=[scalars, pl.BlockSpec((tokens, span), lambda i: (0, 0)), weights, weights],
        out_specs=(pieces, pieces),
        scratch_shapes=[pltpu.VMEM((2, units, tokens), f32)],
        compiler_params=vmem_params(32),
        cost_estimate=cost(4 * tokens * span * units, 4 * span * units),
        name="reference_partials",
    )(place, rows, ref_gate, ref_up)


def match_kernel(refs, columns, numerator, sums, turned):
    tokens, units = columns.shape
    wide = unit_block(units)

    @pl.when(pl.program_id(0) == 0)
    def _():
        for i in range(0, units, wide):
            turned[i : i + wide, :] = columns[:, i : i + wide].T

    rows = refs[...]
    total = jnp.zeros(numerator.shape, f32)
    colsum = jnp.zeros((rows.shape[0], 128), f32)
    weighted = jnp.zeros((rows.shape[0], 128), f32)
    for i in range(0, units, wide):
        r = jnp.dot(rows, columns[:, i : i + wide], preferred_element_type=f32)
        w = jnp.exp2(r * (sharpness * log2_e / tokens))
        total += jnp.dot(w.astype(bf16), turned[i : i + wide, :], preferred_element_type=f32)
        wr = w * r
        for k in range(0, wide, 128):
            colsum += w[:, k : k + 128]
            weighted += wr[:, k : k + 128]
    numerator[...] = total
    sums[0] = jnp.sum(colsum, axis=1, keepdims=True)
    sums[1] = jnp.sum(weighted, axis=1, keepdims=True) * (1.0 / tokens)


def match(refs, columns):
    rows, tokens = refs.shape
    units = columns.shape[1]
    high = 512
    return pl.pallas_call(
        match_kernel,
        grid=(rows // high,),
        out_shape=(
            jax.ShapeDtypeStruct((rows, tokens), f32),
            jax.ShapeDtypeStruct((2, rows, 1), f32),
        ),
        in_specs=[
            pl.BlockSpec((high, tokens), lambda j: (j, 0)),
            pl.BlockSpec((tokens, units), lambda j: (0, 0)),
        ],
        out_specs=(
            pl.BlockSpec((high, tokens), lambda j: (j, 0)),
            pl.BlockSpec((2, high, 1), lambda j: (0, j, 0)),
        ),
        scratch_shapes=[pltpu.VMEM((units, tokens), bf16)],
        compiler_params=vmem_params(32),
        cost_estimate=cost(4 * rows * units * tokens, 8 * rows * tokens, rows * units),
        name="match",
    )(refs, columns)


def place_kernel(place, *refs):
    *pieces, out = refs
    size = pieces[0].shape[0]
    for p, piece in enumerate(pieces):
        at = pl.ds(pl.multiple_of((place[1] ^ p) * size, 8), size)
        out[at, :] = piece[...].astype(f32)


def placed(place, pieces):
    size, tokens = pieces[0].shape
    return pl.pallas_call(
        place_kernel,
        out_shape=jax.ShapeDtypeStruct((size * len(pieces), tokens), f32),
        in_specs=[scalars] + [whole] * len(pieces),
        out_specs=whole,
        compiler_params=vmem_params(16),
        cost_estimate=cost(1e5, 6 * size * len(pieces) * tokens),
        name="placed",
    )(place, *pieces)


def body(clients, parts, token_ids, embed_table, norm_gain, client_gate, client_up, ref_gate, ref_up):
    client = lax.axis_index("client")
    unit = lax.axis_index("unit")
    place = jnp.stack([client * parts + unit, client]).astype(jnp.int32)
    over_clients = functools.partial(xor_permute, axis="client", size=clients)
    over_units = functools.partial(xor_permute, axis="unit", size=parts)

    def gathered(own):
        blocks = [None] * clients
        for p in range(0, clients, 2):
            blocks[p] = over_clients(own, mask=p) if p else own
        for p in range(0, clients, 2):
            blocks[p + 1] = over_clients(blocks[p], mask=1)
        return blocks

    def scattered(keep, send):
        total = keep.astype(f32) + over_clients(send, mask=1).astype(f32)
        arrived = [over_clients(total[p // 2].astype(bf16), mask=p) for p in range(2, clients, 2)]
        mine = total[0]
        for other in arrived:
            mine = mine + other.astype(f32)
        return mine

    keep, send = select_rows(token_ids, place, norm_gain, embed_table, clients)
    own_rows = scattered(keep, send).astype(bf16)
    bit = 1
    while bit < parts:
        own_rows = own_rows + over_units(own_rows, mask=bit)
        bit *= 2

    blocks = gathered(own_rows)
    ref_keep, ref_send = reference_partials(place, own_rows, ref_gate, ref_up, clients)
    pre = scattered(ref_keep, ref_send)
    ref_piece = standardized(gated(pre[0], pre[1]), 1)
    even = range(0, parts, 2)
    ref_pieces = jnp.stack([over_units(ref_piece, mask=k) if k else ref_piece for k in even])
    refs = jnp.stack(gathered(ref_pieces), axis=1)
    groups, _, piece, tokens = refs.shape
    refs = refs.reshape(groups * clients * piece, tokens)

    columns = client_activations(place, blocks, client_gate, client_up)
    other = over_units(columns, mask=1)
    numerator_a, sums_a = match(refs, columns)
    numerator_b, sums_b = match(refs, other)
    sums = (sums_a + sums_b).reshape(2, groups, clients * piece)
    all_sums = sums
    for k in even[1:]:
        theirs = over_units(sums, mask=k)
        all_sums = all_sums + jnp.stack([theirs[:, g ^ (k // 2)] for g in range(groups)], axis=1)
    colsum, weighted = all_sums[0], all_sums[1]
    score = (weighted[0] / colsum[0]).reshape(clients, piece)
    score = score[jnp.arange(clients) ^ client].reshape(1, clients * piece)

    inverse = (1.0 / clients) / colsum
    numerator = (numerator_a + numerator_b).reshape(groups, clients * piece, tokens)
    matched = (numerator * inverse[:, :, None]).astype(bf16)
    matched = matched.reshape(groups, clients // 2, 2, piece, tokens)
    summed = scattered(
        matched[:, :, 0].transpose(1, 0, 2, 3), matched[:, :, 1].transpose(1, 0, 2, 3)
    )
    mine = summed[0]
    for k in even[1:]:
        mine = mine + over_units(summed[k // 2].astype(bf16), mask=k).astype(f32)
    merged = placed(place, gathered(mine.astype(bf16)))
    return (merged, score)


def solution(mesh):
    in_specs = (
        P(),
        P(("client", "unit"), None),
        P(),
        P("client", None, "unit"),
        P("client", None, "unit"),
        P("client", "unit"),
        P("client", "unit"),
    )
    out_specs = (P("unit", None), P("client", "unit"))
    local = functools.partial(body, mesh.shape["client"], mesh.shape["unit"])
    return jax.shard_map(local, mesh=mesh, in_specs=in_specs, out_specs=out_specs, check_vma=False)
```

```python
import functools

import jax
import jax.numpy as jnp
from jax import lax
from jax.experimental import pallas as pl
from jax.experimental.pallas import tpu as pltpu
from jax.sharding import PartitionSpec as P

sharpness = 40.0
log2_e = 1.4426950408889634
group_rows = 16
fetch_slots = 16
bf16 = jnp.bfloat16
f32 = jnp.float32
whole = pl.BlockSpec(memory_space=pltpu.VMEM)
scalars = pl.BlockSpec(memory_space=pltpu.SMEM)
anywhere = pl.BlockSpec(memory_space=pl.ANY)
in_hbm = pl.BlockSpec(memory_space=pltpu.HBM)


def vmem_params(mib):
    return pltpu.CompilerParams(vmem_limit_bytes=mib * 1024 * 1024)


def cost(flops, bytes_accessed, transcendentals=0):
    return pl.CostEstimate(
        flops=int(flops), bytes_accessed=int(bytes_accessed), transcendentals=int(transcendentals)
    )


def xor_permute(value, axis, size, mask):
    return lax.ppermute(value, axis, [(i, i ^ mask) for i in range(size)])


def select_kernel(ids, place, gain, table, keep, send, rows, held, slots, sems):
    tokens, width = rows.shape
    rows_here = table.shape[0]
    start = place[0] * rows_here
    client = place[1]

    def note(t, count):
        local = ids[t] - start
        held[count] = t
        return count + jnp.logical_and(local >= 0, local < rows_here).astype(jnp.int32)

    def fetch(k):
        t = held[k]
        group = pl.multiple_of((ids[t] - start) // group_rows * group_rows, group_rows)
        slot = lax.rem(k, fetch_slots)
        return pltpu.make_async_copy(
            table.at[pl.ds(group, group_rows), :], slots.at[slot], sems.at[slot]
        )

    count = lax.fori_loop(0, tokens, note, jnp.int32(0), unroll=8)

    def begin(k, carry):
        fetch(k).start()
        return carry

    lax.fori_loop(0, jnp.minimum(count, fetch_slots), begin, 0)
    rows[...] = jnp.zeros_like(rows)
    sublane = lax.broadcasted_iota(jnp.int32, (group_rows, width), 0)

    def place_row(k, carry):
        fetch(k).wait()
        t = held[k]
        row_in_group = lax.rem(ids[t] - start, group_rows)
        block = slots[lax.rem(k, fetch_slots)].astype(f32)
        row = jnp.sum(jnp.where(sublane == row_in_group, block, 0.0), axis=0, keepdims=True)
        scale = lax.rsqrt(jnp.sum(row * row, axis=1, keepdims=True) * (1.0 / width) + 1e-05)
        rows[pl.ds(t, 1), :] = row * scale * gain[...]

        @pl.when(k + fetch_slots < count)
        def _():
            fetch(k + fetch_slots).start()

        return carry

    lax.fori_loop(0, count, place_row, 0)
    span = keep.shape[2]
    for p in range(2 * keep.shape[0]):
        source = pl.multiple_of((client ^ p) * span, span)
        target = send if p % 2 else keep
        target[p // 2] = rows[:, pl.ds(source, span)].astype(bf16)


def select_rows(token_ids, place, norm_gain, embed_table, clients):
    tokens, width = token_ids.shape[0], embed_table.shape[1]
    half = jax.ShapeDtypeStruct((clients // 2, tokens, width // clients), bf16)
    return pl.pallas_call(
        select_kernel,
        out_shape=(half, half),
        in_specs=[scalars, scalars, whole, in_hbm],
        out_specs=(whole, whole),
        scratch_shapes=[
            pltpu.VMEM((tokens, width), f32),
            pltpu.SMEM((tokens + 1,), jnp.int32),
            pltpu.VMEM((fetch_slots, group_rows, width), bf16),
            pltpu.SemaphoreType.DMA((fetch_slots,)),
        ],
        compiler_params=vmem_params(48),
        cost_estimate=cost(4e6, 4e6),
        name="select_rows",
    )(token_ids, place, norm_gain[None, :], embed_table)


def standardized(hidden, axis):
    count = hidden.shape[axis]
    center = jnp.sum(hidden, axis=axis, keepdims=True) * (1.0 / count)
    shifted = hidden - center
    spread = jnp.sum(shifted * shifted, axis=axis, keepdims=True) * (1.0 / count)
    return (shifted * lax.rsqrt(spread + 1e-06)).astype(bf16)


def gated(gate, up):
    return gate / (1.0 + jnp.exp(-gate)) * up


def client_kernel(first, place, *refs):
    *blocks, gate_w, up_w, out = refs
    client = place[1]
    tokens, span = blocks[0].shape
    wide = unit_block(gate_w.shape[2])
    for at in range(0, out.shape[1], wide):
        units = slice(first + at, first + at + wide)
        gate = jnp.zeros((tokens, wide), f32)
        up = jnp.zeros((tokens, wide), f32)
        for p, block in enumerate(blocks):
            features = pl.ds(pl.multiple_of((client ^ p) * span, span), span)
            gate += jnp.dot(block[...], gate_w[0, features, units], preferred_element_type=f32)
            up += jnp.dot(block[...], up_w[0, features, units], preferred_element_type=f32)
        out[:, at : at + wide] = standardized(gated(gate, up), 0)


def unit_block(units, most=256):
    return most if units % most == 0 else most // 2


def client_activations(place, blocks, client_gate, client_up, first, last):
    tokens = blocks[0].shape[0]
    width, units = client_gate.shape[1], last - first
    return pl.pallas_call(
        functools.partial(client_kernel, first),
        out_shape=jax.ShapeDtypeStruct((tokens, units), bf16),
        in_specs=[scalars] + [whole] * (len(blocks) + 2),
        out_specs=whole,
        compiler_params=vmem_params(8),
        cost_estimate=cost(4 * tokens * width * units, 4 * width * units),
        name="client_activations",
    )(place, *blocks, client_gate, client_up)


def partial_kernel(place, rows, gate_w, up_w, keep, send, total):
    step = pl.program_id(0)
    wide = gate_w.shape[1]
    at = pl.ds(pl.multiple_of(step * wide, wide), wide)
    total[0, at, :] = jnp.dot(rows[...], gate_w[...], preferred_element_type=f32).T
    total[1, at, :] = jnp.dot(rows[...], up_w[...], preferred_element_type=f32).T

    @pl.when(step == pl.num_programs(0) - 1)
    def _():
        piece = keep.shape[2]
        for p in range(2 * keep.shape[0]):
            source = pl.ds(pl.multiple_of((place[1] ^ p) * piece, 8), piece)
            for which in range(2):
                if p % 2:
                    send[p // 2, which] = total[which, source, :].astype(bf16)
                else:
                    keep[p // 2, which] = total[which, source, :]


def reference_partials(place, rows, ref_gate, ref_up, clients):
    tokens, span = rows.shape
    units = ref_gate.shape[1]
    wide = unit_block(units)
    shape = (clients // 2, 2, units // clients, tokens)
    weights = pl.BlockSpec((span, wide), lambda i: (0, i))
    pieces = pl.BlockSpec(shape, lambda i: (0, 0, 0, 0))
    return pl.pallas_call(
        partial_kernel,
        grid=(units // wide,),
        out_shape=(jax.ShapeDtypeStruct(shape, f32), jax.ShapeDtypeStruct(shape, bf16)),
        in_specs=[scalars, pl.BlockSpec((tokens, span), lambda i: (0, 0)), weights, weights],
        out_specs=(pieces, pieces),
        scratch_shapes=[pltpu.VMEM((2, units, tokens), f32)],
        compiler_params=vmem_params(18),
        cost_estimate=cost(4 * tokens * span * units, 4 * span * units),
        name="reference_partials",
    )(place, rows, ref_gate, ref_up)


def match_kernel(sources, *args):
    refs, *rest = args
    columns, rest = rest[:sources], rest[sources:]
    numerator, sums = rest[-2:]
    tokens = refs.shape[1]
    rows = refs[...]
    if len(rest) > 2:
        total = rest[0][...]
    else:
        total = jnp.zeros(numerator.shape, f32)
    colsum = jnp.zeros((rows.shape[0], 128), f32)
    weighted = jnp.zeros((rows.shape[0], 128), f32)
    for source in columns:
        wide = unit_block(source.shape[1])
        for i in range(0, source.shape[1], wide):
            some = source[:, i : i + wide]
            r = jnp.dot(rows, some, preferred_element_type=f32)
            w = jnp.exp2(r * (sharpness * log2_e / tokens))
            total += lax.dot_general(
                w.astype(bf16), some, (((1,), (1,)), ((), ())), preferred_element_type=f32
            )
            wr = w * r
            for k in range(0, wide, 128):
                colsum += w[:, k : k + 128]
                weighted += wr[:, k : k + 128]
    numerator[...] = total
    row = jnp.sum(colsum.T, axis=0, keepdims=True)
    row_weighted = jnp.sum(weighted.T, axis=0, keepdims=True) * (1.0 / tokens)
    if len(rest) > 2:
        row = row + rest[1][0:1, :]
        row_weighted = row_weighted + rest[1][1:2, :]
    sums[0:1, :] = row
    sums[1:2, :] = row_weighted


def match(refs, columns, before=()):
    rows, tokens = refs.shape
    units = sum(source.shape[1] for source in columns)
    high = 896
    numerators = pl.BlockSpec((high, tokens), lambda j: (j, 0))
    sums = pl.BlockSpec((2, high), lambda j: (0, j))
    return pl.pallas_call(
        functools.partial(match_kernel, len(columns)),
        grid=(rows // high,),
        out_shape=(
            jax.ShapeDtypeStruct((rows, tokens), f32),
            jax.ShapeDtypeStruct((2, rows), f32),
        ),
        in_specs=[numerators]
        + [pl.BlockSpec(source.shape, lambda j: (0, 0)) for source in columns]
        + [numerators, sums][: len(before)],
        out_specs=(numerators, sums),
        compiler_params=vmem_params(20),
        cost_estimate=cost(4 * rows * units * tokens, 8 * rows * tokens, rows * units),
        name="match",
    )(refs, *columns, *before)


def scale_kernel(numerator, factor, keep, send):
    pieces, size = 2 * keep.shape[0], keep.shape[2]
    lanes = 128
    by_row = jnp.broadcast_to(factor[...], (lanes, pieces * size)).T
    for p in range(pieces):
        target = send if p % 2 else keep
        units = slice(p * size, (p + 1) * size)
        for k in range(0, numerator.shape[1], lanes):
            target[p // 2, 0, :, k : k + lanes] = (
                numerator[units, k : k + lanes] * by_row[units]
            ).astype(target.dtype)


def scaled(numerator, factor, clients, groups):
    rows, tokens = numerator.shape
    units = rows // groups
    shape = (clients // 2, groups, units // clients, tokens)
    pieces = pl.BlockSpec((shape[0], 1, shape[2], tokens), lambda g: (0, g, 0, 0))
    return pl.pallas_call(
        scale_kernel,
        grid=(groups,),
        out_shape=(jax.ShapeDtypeStruct(shape, f32), jax.ShapeDtypeStruct(shape, bf16)),
        in_specs=[
            pl.BlockSpec((units, tokens), lambda g: (g, 0)),
            pl.BlockSpec((1, units), lambda g: (0, g)),
        ],
        out_specs=(pieces, pieces),
        compiler_params=vmem_params(20),
        cost_estimate=cost(rows * tokens, 7 * rows * tokens),
        name="scaled",
    )(numerator, factor)


def tie_kernel(value, *rest):
    rest[-1][...] = value[...]


def tied(value, *others):
    return pl.pallas_call(
        tie_kernel,
        out_shape=jax.ShapeDtypeStruct(value.shape, value.dtype),
        in_specs=[whole] + [anywhere] * len(others),
        out_specs=whole,
        compiler_params=vmem_params(8),
        name="tied",
    )(value, *others)


def place_kernel(place, *refs):
    *pieces, out = refs
    size = pieces[0].shape[0]
    for p, piece in enumerate(pieces):
        at = pl.ds(pl.multiple_of((place[1] ^ p) * size, 8), size)
        out[at, :] = piece[...].astype(f32)


def placed(place, pieces):
    size, tokens = pieces[0].shape
    return pl.pallas_call(
        place_kernel,
        out_shape=jax.ShapeDtypeStruct((size * len(pieces), tokens), f32),
        in_specs=[scalars] + [whole] * len(pieces),
        out_specs=whole,
        compiler_params=vmem_params(16),
        cost_estimate=cost(1e5, 6 * size * len(pieces) * tokens),
        name="placed",
    )(place, *pieces)


def body(clients, parts, token_ids, embed_table, norm_gain, client_gate, client_up, ref_gate, ref_up):
    client = lax.axis_index("client")
    unit = lax.axis_index("unit")
    place = jnp.stack([client * parts + unit, client]).astype(jnp.int32)
    over_clients = functools.partial(xor_permute, axis="client", size=clients)
    over_units = functools.partial(xor_permute, axis="unit", size=parts)

    def gathered(own, after=()):
        blocks = [own] + [None] * (clients - 1)
        far = tied(own, *after) if after else own
        for p in range(2, clients, 2):
            blocks[p] = over_clients(far, mask=p)
        for p in range(0, clients, 2):
            blocks[p + 1] = over_clients(blocks[p], mask=1)
        return blocks

    def summed_pairs(keep, send):
        return keep.astype(f32) + over_clients(send, mask=1).astype(f32)

    def sent(total):
        return [over_clients(total[p // 2].astype(bf16), mask=p) for p in range(2, clients, 2)]

    def summed(total, arrived):
        mine = total[0]
        for other in arrived:
            mine = mine + other.astype(f32)
        return mine

    keep, send = select_rows(token_ids, place, norm_gain, embed_table, clients)
    total = summed_pairs(keep, send)
    half = total.shape[1] // 2
    halves = [total[:, :half], total[:, half:]]
    halves = [(part, sent(part)) for part in halves]
    halves = [summed(*part).astype(bf16) for part in halves]
    bit = 1
    while bit < parts:
        halves = [part + over_units(part, mask=bit) for part in halves]
        bit *= 2
    own_rows = jnp.concatenate(halves, axis=0)

    ref_keep, ref_send = reference_partials(place, own_rows, ref_gate, ref_up, clients)
    total = summed_pairs(ref_keep, ref_send)
    arrived = sent(total)
    blocks = gathered(own_rows, [total])
    pre = summed(total, arrived)
    ref_piece = standardized(gated(pre[0], pre[1]), 1)
    even = range(0, parts, 2)
    groups, (piece, tokens) = len(even), ref_piece.shape
    ref_pieces = jnp.stack([over_units(ref_piece, mask=k) if k else ref_piece for k in even])
    refs = jnp.stack(gathered(ref_pieces), axis=1).reshape(groups * clients * piece, tokens)

    units = client_gate.shape[2]
    cuts = [0, 2 * units // 7, 5 * units // 7, units]
    own = [
        client_activations(place, blocks, client_gate, client_up, first, last)
        for first, last in zip(cuts, cuts[1:])
    ]
    theirs = [over_units(part, mask=1) for part in own]
    sofar = match(refs, own)
    for part in theirs:
        sofar = match(refs, [part], sofar)
    numerator, sums = sofar
    sums = sums.reshape(2, groups, clients * piece)
    all_sums = sums
    for k in even[1:]:
        other = over_units(sums, mask=k)
        all_sums = all_sums + jnp.stack([other[:, g ^ (k // 2)] for g in range(groups)], axis=1)
    colsum, weighted = all_sums[0], all_sums[1]
    score = (weighted[0] / colsum[0]).reshape(clients, piece)
    here = jnp.arange(clients)[:, None] ^ client == jnp.arange(clients)[None, :]
    score = jnp.sum(jnp.where(here[:, :, None], score[None], 0.0), axis=1)
    score = score.reshape(1, clients * piece)

    inverse = ((1.0 / clients) / colsum).reshape(1, groups * clients * piece)
    total = summed_pairs(*scaled(numerator, inverse, clients, groups))
    reduced = summed(total, sent(total))
    mine = reduced[0]
    for k in even[1:]:
        mine = mine + over_units(reduced[k // 2].astype(bf16), mask=k).astype(f32)
    merged = placed(place, gathered(mine.astype(bf16)))
    return (merged, score)


def solution(mesh):
    in_specs = (
        P(),
        P(("client", "unit"), None),
        P(),
        P("client", None, "unit"),
        P("client", None, "unit"),
        P("client", "unit"),
        P("client", "unit"),
    )
    out_specs = (P("unit", None), P("client", "unit"))
    local = functools.partial(body, mesh.shape["client"], mesh.shape["unit"])
    return jax.shard_map(local, mesh=mesh, in_specs=in_specs, out_specs=out_specs, check_vma=False)
```

```python
import functools

import jax
import jax.numpy as jnp
from jax import lax
from jax.experimental import pallas as pl
from jax.experimental.pallas import tpu as pltpu
from jax.sharding import PartitionSpec as P

sharpness = 40.0
log2_e = 1.4426950408889634
group_rows = 16
fetch_slots = 16
bf16 = jnp.bfloat16
f32 = jnp.float32
whole = pl.BlockSpec(memory_space=pltpu.VMEM)
scalars = pl.BlockSpec(memory_space=pltpu.SMEM)
anywhere = pl.BlockSpec(memory_space=pl.ANY)
in_hbm = pl.BlockSpec(memory_space=pltpu.HBM)


def vmem_params(mib):
    return pltpu.CompilerParams(vmem_limit_bytes=mib * 1024 * 1024)


def cost(flops, bytes_accessed, transcendentals=0):
    return pl.CostEstimate(
        flops=int(flops), bytes_accessed=int(bytes_accessed), transcendentals=int(transcendentals)
    )


def xor_permute(value, axis, size, mask):
    return lax.ppermute(value, axis, [(i, i ^ mask) for i in range(size)])


def select_kernel(place, ids_far, gain_far, table, keep, send, ids, gain, rows, held, slots, sems, first):
    arrivals = [
        pltpu.make_async_copy(ids_far, ids, first.at[0]),
        pltpu.make_async_copy(gain_far, gain, first.at[1]),
    ]
    for arrival in arrivals:
        arrival.start()
    for arrival in arrivals:
        arrival.wait()
    tokens, width = rows.shape
    rows_here = table.shape[0]
    start = place[0] * rows_here
    client = place[1]

    def note(t, count):
        local = ids[t] - start
        held[count] = t
        return count + jnp.logical_and(local >= 0, local < rows_here).astype(jnp.int32)

    def fetch(k):
        t = held[k]
        group = pl.multiple_of((ids[t] - start) // group_rows * group_rows, group_rows)
        slot = lax.rem(k, fetch_slots)
        return pltpu.make_async_copy(
            table.at[pl.ds(group, group_rows), :], slots.at[slot], sems.at[slot]
        )

    count = lax.fori_loop(0, tokens, note, jnp.int32(0), unroll=8)

    def begin(k, carry):
        fetch(k).start()
        return carry

    lax.fori_loop(0, jnp.minimum(count, fetch_slots), begin, 0)
    rows[...] = jnp.zeros_like(rows)
    sublane = lax.broadcasted_iota(jnp.int32, (group_rows, width), 0)

    def place_row(k, carry):
        fetch(k).wait()
        t = held[k]
        row_in_group = lax.rem(ids[t] - start, group_rows)
        block = slots[lax.rem(k, fetch_slots)].astype(f32)
        row = jnp.sum(jnp.where(sublane == row_in_group, block, 0.0), axis=0, keepdims=True)
        scale = lax.rsqrt(jnp.sum(row * row, axis=1, keepdims=True) * (1.0 / width) + 1e-05)
        rows[pl.ds(t, 1), :] = row * scale * gain[...]

        @pl.when(k + fetch_slots < count)
        def _():
            fetch(k + fetch_slots).start()

        return carry

    lax.fori_loop(0, count, place_row, 0)
    span = keep.shape[2]
    for p in range(2 * keep.shape[0]):
        source = pl.multiple_of((client ^ p) * span, span)
        target = send if p % 2 else keep
        target[p // 2] = rows[:, pl.ds(source, span)].astype(bf16)


def select_rows(token_ids, place, norm_gain, embed_table, clients):
    tokens, width = token_ids.shape[0], embed_table.shape[1]
    half = jax.ShapeDtypeStruct((clients // 2, tokens, width // clients), bf16)
    return pl.pallas_call(
        select_kernel,
        out_shape=(half, half),
        in_specs=[scalars, in_hbm, in_hbm, in_hbm],
        out_specs=(whole, whole),
        scratch_shapes=[
            pltpu.SMEM((tokens,), jnp.int32),
            pltpu.VMEM((1, width), f32),
            pltpu.VMEM((tokens, width), f32),
            pltpu.SMEM((tokens + 1,), jnp.int32),
            pltpu.VMEM((fetch_slots, group_rows, width), bf16),
            pltpu.SemaphoreType.DMA((fetch_slots,)),
            pltpu.SemaphoreType.DMA((2,)),
        ],
        compiler_params=vmem_params(48),
        cost_estimate=cost(4e6, 4e6),
        name="select_rows",
    )(place, token_ids, norm_gain[None, :], embed_table)


def standardized(hidden, axis):
    count = hidden.shape[axis]
    center = jnp.sum(hidden, axis=axis, keepdims=True) * (1.0 / count)
    shifted = hidden - center
    spread = jnp.sum(shifted * shifted, axis=axis, keepdims=True) * (1.0 / count)
    return (shifted * lax.rsqrt(spread + 1e-06)).astype(bf16)


def gated(gate, up):
    return gate / (1.0 + jnp.exp(-gate)) * up


def client_kernel(first, place, *refs):
    *blocks, gate_w, up_w, out = refs
    client = place[1]
    tokens, span = blocks[0].shape
    wide = out.shape[1]
    units = pl.ds(pl.multiple_of((first + pl.program_id(0)) * wide, wide), wide)
    gate = jnp.zeros((tokens, wide), f32)
    up = jnp.zeros((tokens, wide), f32)
    for p, block in enumerate(blocks):
        features = pl.ds(pl.multiple_of((client ^ p) * span, span), span)
        gate += jnp.dot(block[...], gate_w[0, features, :], preferred_element_type=f32)
        up += jnp.dot(block[...], up_w[0, features, units], preferred_element_type=f32)
    out[...] = standardized(gated(gate, up), 0)


def client_activations(place, blocks, client_gate, client_up, first, last):
    tokens = blocks[0].shape[0]
    width, units = client_gate.shape[1], last - first
    wide = unit_block(client_gate.shape[2])
    start = first // wide
    return pl.pallas_call(
        functools.partial(client_kernel, start),
        grid=(units // wide,),
        out_shape=jax.ShapeDtypeStruct((tokens, units), bf16),
        in_specs=[scalars]
        + [whole] * len(blocks)
        + [pl.BlockSpec((1, width, wide), lambda i: (0, 0, start + i)), whole],
        out_specs=pl.BlockSpec((tokens, wide), lambda i: (0, i)),
        compiler_params=vmem_params(12),
        cost_estimate=cost(4 * tokens * width * units, 4 * width * units),
        name="client_activations",
    )(place, *blocks, client_gate, client_up)


def unit_block(units, most=256):
    return most if units % most == 0 else most // 2


def partial_kernel(place, rows, gate_w, up_w, keep, send, total):
    wide = unit_block(gate_w.shape[1])
    for which, weights in enumerate((gate_w, up_w)):
        for at in range(0, weights.shape[1], wide):
            total[which, at : at + wide, :] = lax.dot_general(
                weights[:, at : at + wide],
                rows[...],
                (((0,), (1,)), ((), ())),
                preferred_element_type=f32,
            )
    piece = keep.shape[2]
    for p in range(2 * keep.shape[0]):
        source = pl.ds(pl.multiple_of((place[1] ^ p) * piece, 8), piece)
        for which in range(2):
            if p % 2:
                send[p // 2, which] = total[which, source, :].astype(bf16)
            else:
                keep[p // 2, which] = total[which, source, :]


def reference_partials(place, rows, ref_gate, ref_up, clients):
    tokens, span = rows.shape
    units = ref_gate.shape[1]
    shape = (clients // 2, 2, units // clients, tokens)
    return pl.pallas_call(
        partial_kernel,
        out_shape=(jax.ShapeDtypeStruct(shape, f32), jax.ShapeDtypeStruct(shape, bf16)),
        in_specs=[scalars] + [whole] * 3,
        out_specs=(whole, whole),
        scratch_shapes=[pltpu.VMEM((2, units, tokens), f32)],
        compiler_params=vmem_params(16),
        cost_estimate=cost(4 * tokens * span * units, 4 * span * units),
        name="reference_partials",
    )(place, rows, ref_gate, ref_up)


def matched(rows, columns, total, with_sums):
    tokens = rows.shape[1]
    colsum = jnp.zeros((rows.shape[0], 128), f32)
    weighted = jnp.zeros((rows.shape[0], 128), f32)
    for source in columns:
        wide = unit_block(source.shape[1])
        for i in range(0, source.shape[1], wide):
            some = source[:, i : i + wide]
            r = jnp.dot(rows, some, preferred_element_type=f32)
            w = jnp.exp2(r * (sharpness * log2_e / tokens))
            if total is not None:
                total += lax.dot_general(
                    w.astype(bf16), some, (((1,), (1,)), ((), ())), preferred_element_type=f32
                )
            if with_sums:
                wr = w * r
                for k in range(0, wide, 128):
                    colsum += w[:, k : k + 128]
                    weighted += wr[:, k : k + 128]
    if not with_sums:
        return total
    row = jnp.sum(colsum.T, axis=0, keepdims=True)
    row_weighted = jnp.sum(weighted.T, axis=0, keepdims=True) * (1.0 / tokens)
    return total, row, row_weighted


def match_kernel(sources, refs, *rest):
    columns, rest = rest[:sources], rest[sources:]
    numerator, sums = rest[-2:]
    before = rest[:-2]
    start = before[0][...] if before else jnp.zeros(numerator.shape, f32)
    total, row, row_weighted = matched(refs[...], columns, start, True)
    numerator[...] = total
    if before:
        row = row + before[1][0:1, :]
        row_weighted = row_weighted + before[1][1:2, :]
    sums[0:1, :] = row
    sums[1:2, :] = row_weighted


def match_last_kernel(refs, columns, before, sums_before, keep, send, sums):
    total, row, row_weighted = matched(refs[...], [columns], before[...], True)
    row = row + sums_before[0:1, :]
    sums[0:1, :] = row
    sums[1:2, :] = row_weighted + sums_before[1:2, :]
    lanes = 128
    by_row = jnp.broadcast_to(1.0 / row, (lanes, total.shape[0])).T
    size = keep.shape[2]
    for p in range(2 * keep.shape[0]):
        target = send if p % 2 else keep
        units = slice(p * size, (p + 1) * size)
        for k in range(0, total.shape[1], lanes):
            target[p // 2, 0, :, k : k + lanes] = (total[units, k : k + lanes] * by_row[units]).astype(
                target.dtype
            )


def join_kernel(keep, arrived, factor, factor_arrived, first, others):
    pairs, groups, size, tokens = keep.shape
    lanes = 128
    units = 2 * pairs * size
    for g in range(groups):
        rows = [
            jnp.broadcast_to(source[:, g * units : (g + 1) * units], (lanes, units)).T
            for source in (factor, factor_arrived)
        ]
        for h in range(pairs):
            ours = slice(2 * h * size, (2 * h + 1) * size)
            theirs = slice((2 * h + 1) * size, (2 * h + 2) * size)
            for k in range(0, tokens, lanes):
                at = slice(k, k + lanes)
                total = keep[h, g, :, at].astype(f32) * rows[0][ours]
                total += arrived[h, g, :, at].astype(f32) * rows[1][theirs]
                if h:
                    others[h - 1, g, :, at] = total.astype(bf16)
                else:
                    first[g, :, at] = total


def joined(keep, arrived, factor, factor_arrived):
    pairs, groups, size, tokens = keep.shape
    return pl.pallas_call(
        join_kernel,
        out_shape=(
            jax.ShapeDtypeStruct((groups, size, tokens), f32),
            jax.ShapeDtypeStruct((pairs - 1, groups, size, tokens), bf16),
        ),
        in_specs=[whole] * 4,
        out_specs=(whole, whole),
        compiler_params=vmem_params(16),
        cost_estimate=cost(4 * keep.size, 6 * keep.size),
        name="joined",
    )(keep, arrived, factor, factor_arrived)


high = 896


def match_cost(rows, tokens, units):
    return cost(4 * rows * units * tokens, 8 * rows * tokens, rows * units)


def by_rows(width):
    return pl.BlockSpec((high, width), lambda j: (j, 0))


def by_columns(rows):
    return pl.BlockSpec((rows, high), lambda j: (0, j))


def unblocked(value):
    return pl.BlockSpec(value.shape, lambda j: (0, 0))


def match(refs, columns, before=()):
    rows, tokens = refs.shape
    units = sum(source.shape[1] for source in columns)
    return pl.pallas_call(
        functools.partial(match_kernel, len(columns)),
        grid=(rows // high,),
        out_shape=(
            jax.ShapeDtypeStruct((rows, tokens), f32),
            jax.ShapeDtypeStruct((2, rows), f32),
        ),
        in_specs=[by_rows(tokens)]
        + [unblocked(source) for source in columns]
        + [by_rows(tokens), by_columns(2)][: len(before)],
        out_specs=(by_rows(tokens), by_columns(2)),
        compiler_params=vmem_params(20),
        cost_estimate=match_cost(rows, tokens, units),
        name="match",
    )(refs, *columns, *before)


def match_last(refs, columns, before, sums, clients, groups):
    rows, tokens = refs.shape
    size = rows // groups // clients
    steps = rows // groups // high
    pairs = max(1, clients // 2 // steps)
    shape = (clients // 2, groups, size, tokens)
    pieces = pl.BlockSpec((pairs, 1, size, tokens), lambda j: (j % steps, j // steps, 0, 0))
    halves = jax.ShapeDtypeStruct(shape, bf16)
    return pl.pallas_call(
        match_last_kernel,
        grid=(rows // high,),
        out_shape=(halves, halves, jax.ShapeDtypeStruct((2, rows), f32)),
        in_specs=[by_rows(tokens), unblocked(columns), by_rows(tokens), by_columns(2)],
        out_specs=(pieces, pieces, by_columns(2)),
        compiler_params=vmem_params(20),
        cost_estimate=match_cost(rows, tokens, columns.shape[1]),
        name="match_last",
    )(refs, columns, before, sums)


def tie_kernel(value, *rest):
    rest[-1][...] = value[...]


def tied(value, *others):
    return pl.pallas_call(
        tie_kernel,
        out_shape=jax.ShapeDtypeStruct(value.shape, value.dtype),
        in_specs=[whole] + [anywhere] * len(others),
        out_specs=whole,
        compiler_params=vmem_params(8),
        name="tied",
    )(value, *others)


def place_kernel(place, *refs):
    *pieces, out = refs
    size = pieces[0].shape[0]
    for p, piece in enumerate(pieces):
        at = pl.ds(pl.multiple_of((place[1] ^ p) * size, 8), size)
        out[at, :] = piece[...].astype(f32)


def placed(place, pieces):
    size, tokens = pieces[0].shape
    return pl.pallas_call(
        place_kernel,
        out_shape=jax.ShapeDtypeStruct((size * len(pieces), tokens), f32),
        in_specs=[scalars] + [whole] * len(pieces),
        out_specs=whole,
        compiler_params=vmem_params(16),
        cost_estimate=cost(1e5, 6 * size * len(pieces) * tokens),
        name="placed",
    )(place, *pieces)


def body(clients, parts, token_ids, embed_table, norm_gain, client_gate, client_up, ref_gate, ref_up):
    client = lax.axis_index("client")
    unit = lax.axis_index("unit")
    place = jnp.stack([client * parts + unit, client]).astype(jnp.int32)
    over_clients = functools.partial(xor_permute, axis="client", size=clients)
    over_units = functools.partial(xor_permute, axis="unit", size=parts)

    def gathered(own, after=()):
        blocks = [own] + [None] * (clients - 1)
        far = tied(own, *after) if after else own
        for p in range(2, clients, 2):
            blocks[p] = over_clients(far, mask=p)
        for p in range(0, clients, 2):
            blocks[p + 1] = over_clients(blocks[p], mask=1)
        return blocks

    def summed_pairs(keep, send):
        return keep.astype(f32) + over_clients(send, mask=1).astype(f32)

    def sent(total):
        return [over_clients(total[p // 2].astype(bf16), mask=p) for p in range(2, clients, 2)]

    def summed(total, arrived):
        mine = total[0]
        for other in arrived:
            mine = mine + other.astype(f32)
        return mine

    keep, send = select_rows(token_ids, place, norm_gain, embed_table, clients)
    total = summed_pairs(keep, send)
    half = total.shape[1] // 2
    halves = [total[:, :half], total[:, half:]]
    halves = [(part, sent(part)) for part in halves]
    halves = [summed(*part).astype(bf16) for part in halves]
    bit = 1
    while bit < parts:
        halves = [part + over_units(part, mask=bit) for part in halves]
        bit *= 2
    own_rows = jnp.concatenate(halves, axis=0)

    ref_keep, ref_send = reference_partials(place, own_rows, ref_gate, ref_up, clients)
    total = summed_pairs(ref_keep, ref_send)
    arrived = sent(total)
    blocks = gathered(own_rows, [total])
    pre = summed(total, arrived)
    ref_piece = standardized(gated(pre[0], pre[1]), 1)
    even = range(0, parts, 2)
    groups, (piece, tokens) = len(even), ref_piece.shape
    ref_pieces = jnp.stack([over_units(ref_piece, mask=k) if k else ref_piece for k in even])
    refs = jnp.stack(gathered(ref_pieces), axis=1).reshape(groups * clients * piece, tokens)

    units = client_gate.shape[2]
    cuts = [0, 5 * units // 7, units]
    own = [
        client_activations(place, blocks, client_gate, client_up, first, last)
        for first, last in zip(cuts, cuts[1:])
    ]
    theirs = [over_units(part, mask=1) for part in own]
    numerator, sums = match(refs, own)
    numerator, sums = match(refs, theirs[:1], (numerator, sums))
    keep, send, sums = match_last(refs, theirs[1], numerator, sums, clients, groups)
    arrived = over_clients(send, mask=1)
    sums = sums.reshape(2, groups, clients * piece)
    all_sums = sums
    for k in even[1:]:
        other = over_units(sums, mask=k)
        all_sums = all_sums + jnp.stack([other[:, g ^ (k // 2)] for g in range(groups)], axis=1)
    colsum, weighted = all_sums[0], all_sums[1]
    factor = (sums[0] * (1.0 / clients) / colsum).reshape(1, groups * clients * piece)
    first, others = joined(keep, arrived, factor, over_clients(factor, mask=1))
    arrived = [over_clients(others[p // 2 - 1], mask=p) for p in range(2, clients, 2)]
    reduced = first
    for other in arrived:
        reduced = reduced + other.astype(f32)

    score = (weighted[0] / colsum[0]).reshape(clients, piece)
    here = jnp.arange(clients)[:, None] ^ client == jnp.arange(clients)[None, :]
    score = jnp.sum(jnp.where(here[:, :, None], score[None], 0.0), axis=1)
    score = score.reshape(1, clients * piece)

    mine = reduced[0]
    for k in even[1:]:
        mine = mine + over_units(reduced[k // 2].astype(bf16), mask=k).astype(f32)
    merged = placed(place, gathered(mine.astype(bf16)))
    return (merged, score)


def solution(mesh):
    in_specs = (
        P(),
        P(("client", "unit"), None),
        P(),
        P("client", None, "unit"),
        P("client", None, "unit"),
        P("client", "unit"),
        P("client", "unit"),
    )
    out_specs = (P("unit", None), P("client", "unit"))
    local = functools.partial(body, mesh.shape["client"], mesh.shape["unit"])
    return jax.shard_map(local, mesh=mesh, in_specs=in_specs, out_specs=out_specs, check_vma=False)
```

```python
import functools

import jax
import jax.numpy as jnp
from jax import lax
from jax.experimental import pallas as pl
from jax.experimental.pallas import tpu as pltpu
from jax.sharding import PartitionSpec as P

sharpness = 40.0
log2_e = 1.4426950408889634
group_rows = 16
fetch_slots = 16
bf16 = jnp.bfloat16
f32 = jnp.float32
whole = pl.BlockSpec(memory_space=pltpu.VMEM)
scalars = pl.BlockSpec(memory_space=pltpu.SMEM)
anywhere = pl.BlockSpec(memory_space=pl.ANY)
in_hbm = pl.BlockSpec(memory_space=pltpu.HBM)


def vmem_params(mib):
    return pltpu.CompilerParams(vmem_limit_bytes=mib * 1024 * 1024)


def cost(flops, bytes_accessed, transcendentals=0):
    return pl.CostEstimate(
        flops=int(flops), bytes_accessed=int(bytes_accessed), transcendentals=int(transcendentals)
    )


def xor_permute(value, axis, size, mask):
    return lax.ppermute(value, axis, [(i, i ^ mask) for i in range(size)])


def select_kernel(place, ids_far, gain_far, table, keep, send, ids, gain, rows, held, slots, sems, first):
    arrivals = [
        pltpu.make_async_copy(ids_far, ids, first.at[0]),
        pltpu.make_async_copy(gain_far, gain, first.at[1]),
    ]
    for arrival in arrivals:
        arrival.start()
    for arrival in arrivals:
        arrival.wait()
    tokens, width = rows.shape
    rows_here = table.shape[0]
    start = place[0] * rows_here
    client = place[1]

    def note(t, count):
        local = ids[t] - start
        held[count] = t
        return count + jnp.logical_and(local >= 0, local < rows_here).astype(jnp.int32)

    def fetch(k):
        t = held[k]
        group = pl.multiple_of((ids[t] - start) // group_rows * group_rows, group_rows)
        slot = lax.rem(k, fetch_slots)
        return pltpu.make_async_copy(
            table.at[pl.ds(group, group_rows), :], slots.at[slot], sems.at[slot]
        )

    count = lax.fori_loop(0, tokens, note, jnp.int32(0), unroll=8)

    def begin(k, carry):
        fetch(k).start()
        return carry

    lax.fori_loop(0, jnp.minimum(count, fetch_slots), begin, 0)
    rows[...] = jnp.zeros_like(rows)
    sublane = lax.broadcasted_iota(jnp.int32, (group_rows, width), 0)

    def place_row(k, carry):
        fetch(k).wait()
        t = held[k]
        row_in_group = lax.rem(ids[t] - start, group_rows)
        block = slots[lax.rem(k, fetch_slots)].astype(f32)
        row = jnp.sum(jnp.where(sublane == row_in_group, block, 0.0), axis=0, keepdims=True)
        scale = lax.rsqrt(jnp.sum(row * row, axis=1, keepdims=True) * (1.0 / width) + 1e-05)
        rows[pl.ds(t, 1), :] = row * scale * gain[...]

        @pl.when(k + fetch_slots < count)
        def _():
            fetch(k + fetch_slots).start()

        return carry

    lax.fori_loop(0, count, place_row, 0)
    span = keep.shape[2]
    for p in range(2 * keep.shape[0]):
        source = pl.multiple_of((client ^ p) * span, span)
        target = send if p % 2 else keep
        target[p // 2] = rows[:, pl.ds(source, span)].astype(bf16)


def select_rows(token_ids, place, norm_gain, embed_table, clients):
    tokens, width = token_ids.shape[0], embed_table.shape[1]
    half = jax.ShapeDtypeStruct((clients // 2, tokens, width // clients), bf16)
    return pl.pallas_call(
        select_kernel,
        out_shape=(half, half),
        in_specs=[scalars, in_hbm, in_hbm, in_hbm],
        out_specs=(whole, whole),
        scratch_shapes=[
            pltpu.SMEM((tokens,), jnp.int32),
            pltpu.VMEM((1, width), f32),
            pltpu.VMEM((tokens, width), f32),
            pltpu.SMEM((tokens + 1,), jnp.int32),
            pltpu.VMEM((fetch_slots, group_rows, width), bf16),
            pltpu.SemaphoreType.DMA((fetch_slots,)),
            pltpu.SemaphoreType.DMA((2,)),
        ],
        compiler_params=vmem_params(48),
        cost_estimate=cost(4e6, 4e6),
        name="select_rows",
    )(place, token_ids, norm_gain[None, :], embed_table)


def standardized(hidden, axis):
    count = hidden.shape[axis]
    center = jnp.sum(hidden, axis=axis, keepdims=True) * (1.0 / count)
    shifted = hidden - center
    spread = jnp.sum(shifted * shifted, axis=axis, keepdims=True) * (1.0 / count)
    return (shifted * lax.rsqrt(spread + 1e-06)).astype(bf16)


def gated(gate, up):
    return gate / (1.0 + jnp.exp(-gate)) * up


def client_kernel(first, place, *refs):
    *blocks, gate_w, up_w, out = refs
    client = place[1]
    tokens, span = blocks[0].shape
    wide = out.shape[1]
    units = pl.ds(pl.multiple_of((first + pl.program_id(0)) * wide, wide), wide)
    gate = jnp.zeros((tokens, wide), f32)
    up = jnp.zeros((tokens, wide), f32)
    for p, block in enumerate(blocks):
        features = pl.ds(pl.multiple_of((client ^ p) * span, span), span)
        gate += jnp.dot(block[...], gate_w[0, features, :], preferred_element_type=f32)
        up += jnp.dot(block[...], up_w[0, features, units], preferred_element_type=f32)
    out[...] = standardized(gated(gate, up), 0)


def client_activations(place, blocks, client_gate, client_up, first, last):
    tokens = blocks[0].shape[0]
    width, units = client_gate.shape[1], last - first
    wide = unit_block(client_gate.shape[2])
    start = first // wide
    return pl.pallas_call(
        functools.partial(client_kernel, start),
        grid=(units // wide,),
        out_shape=jax.ShapeDtypeStruct((tokens, units), bf16),
        in_specs=[scalars]
        + [whole] * len(blocks)
        + [pl.BlockSpec((1, width, wide), lambda i: (0, 0, start + i)), whole],
        out_specs=pl.BlockSpec((tokens, wide), lambda i: (0, i)),
        compiler_params=vmem_params(12),
        cost_estimate=cost(4 * tokens * width * units, 4 * width * units),
        name="client_activations",
    )(place, *blocks, client_gate, client_up)


def unit_block(units, most=256):
    return most if units % most == 0 else most // 2


def partial_kernel(place, rows, gate_w, up_w, keep, send, total):
    wide = unit_block(gate_w.shape[1])
    for which, weights in enumerate((gate_w, up_w)):
        for at in range(0, weights.shape[1], wide):
            total[which, at : at + wide, :] = lax.dot_general(
                weights[:, at : at + wide],
                rows[...],
                (((0,), (1,)), ((), ())),
                preferred_element_type=f32,
            )
    piece = keep.shape[2]
    for p in range(2 * keep.shape[0]):
        source = pl.ds(pl.multiple_of((place[1] ^ p) * piece, 8), piece)
        for which in range(2):
            if p % 2:
                send[p // 2, which] = total[which, source, :].astype(bf16)
            else:
                keep[p // 2, which] = total[which, source, :]


def reference_partials(place, rows, ref_gate, ref_up, clients):
    tokens, span = rows.shape
    units = ref_gate.shape[1]
    shape = (clients // 2, 2, units // clients, tokens)
    return pl.pallas_call(
        partial_kernel,
        out_shape=(jax.ShapeDtypeStruct(shape, f32), jax.ShapeDtypeStruct(shape, bf16)),
        in_specs=[scalars] + [whole] * 3,
        out_specs=(whole, whole),
        scratch_shapes=[pltpu.VMEM((2, units, tokens), f32)],
        compiler_params=vmem_params(16),
        cost_estimate=cost(4 * tokens * span * units, 4 * span * units),
        name="reference_partials",
    )(place, rows, ref_gate, ref_up)


def matched(rows, columns, total):
    tokens = rows.shape[1]
    colsum = jnp.zeros((rows.shape[0], 128), f32)
    for source in columns:
        wide = unit_block(source.shape[1])
        for i in range(0, source.shape[1], wide):
            some = source[:, i : i + wide]
            r = jnp.dot(rows, some, preferred_element_type=f32)
            w = jnp.exp2(r * (sharpness * log2_e / tokens))
            total += lax.dot_general(
                w.astype(bf16), some, (((1,), (1,)), ((), ())), preferred_element_type=f32
            )
            for k in range(0, wide, 128):
                colsum += w[:, k : k + 128]
    return total, jnp.sum(colsum.T, axis=0, keepdims=True)


def match_kernel(sources, refs, *rest):
    columns, rest = rest[:sources], rest[sources:]
    numerator, sums = rest[-2:]
    before = rest[:-2]
    start = before[0][...] if before else jnp.zeros(numerator.shape, f32)
    numerator[...], row = matched(refs[...], columns, start)
    sums[...] = row + before[1][...] if before else row


def match_last_kernel(refs, columns, before, sums_before, keep, send, sums):
    total, row = matched(refs[...], [columns], before[...])
    tokens, lanes = total.shape[1], 128
    row = row + sums_before[...]
    sums[0:1, :] = row
    weighted = total * refs[...].astype(f32)
    weighted = sum(weighted[:, k : k + lanes] for k in range(0, tokens, lanes))
    sums[1:2, :] = jnp.sum(weighted.T, axis=0, keepdims=True) * (1.0 / tokens)
    by_row = jnp.broadcast_to(1.0 / row, (lanes, total.shape[0])).T
    size = keep.shape[2]
    for p in range(2 * keep.shape[0]):
        target = send if p % 2 else keep
        units = slice(p * size, (p + 1) * size)
        for k in range(0, tokens, lanes):
            target[p // 2, 0, :, k : k + lanes] = (total[units, k : k + lanes] * by_row[units]).astype(
                target.dtype
            )


def join_kernel(group, keep, arrived, factor, factor_arrived, *refs):
    pairs, _, size, tokens = keep.shape
    first, *others = refs[-pairs:]
    lanes = 128
    units = 2 * pairs * size
    rows = [
        jnp.broadcast_to(source[:, group * units : (group + 1) * units], (lanes, units)).T
        for source in (factor, factor_arrived)
    ]
    for h in range(pairs):
        ours = slice(2 * h * size, (2 * h + 1) * size)
        theirs = slice((2 * h + 1) * size, (2 * h + 2) * size)
        for k in range(0, tokens, lanes):
            at = slice(k, k + lanes)
            total = keep[h, group, :, at].astype(f32) * rows[0][ours]
            total += arrived[h, group, :, at].astype(f32) * rows[1][theirs]
            if h:
                others[h - 1][:, at] = total.astype(bf16)
            else:
                first[:, at] = total


def joined(group, keep, arrived, factor, factor_arrived, after):
    pairs, _, size, tokens = keep.shape
    piece = jax.ShapeDtypeStruct((size, tokens), bf16)
    return pl.pallas_call(
        functools.partial(join_kernel, group),
        out_shape=(jax.ShapeDtypeStruct((size, tokens), f32), *[piece] * (pairs - 1)),
        in_specs=[whole] * 4 + [anywhere] * len(after),
        out_specs=(whole,) * pairs,
        compiler_params=vmem_params(16),
        cost_estimate=cost(4 * pairs * size * tokens, 6 * pairs * size * tokens),
        name="joined",
    )(keep, arrived, factor, factor_arrived, *after)


def match_cost(rows, tokens, units):
    return cost(4 * rows * units * tokens, 8 * rows * tokens, rows * units)


def match_specs(rows, tokens, groups):
    high = rows // groups
    by_rows = pl.BlockSpec((high, tokens), lambda j: (j, 0))
    return by_rows, *[pl.BlockSpec((n, high), lambda j: (0, j)) for n in (1, 2)]


def unblocked(value):
    return pl.BlockSpec(value.shape, lambda j: (0, 0))


def match(refs, columns, groups, before=()):
    rows, tokens = refs.shape
    units = sum(source.shape[1] for source in columns)
    by_rows, one_row, _ = match_specs(rows, tokens, groups)
    return pl.pallas_call(
        functools.partial(match_kernel, len(columns)),
        grid=(groups,),
        out_shape=(
            jax.ShapeDtypeStruct((rows, tokens), f32),
            jax.ShapeDtypeStruct((1, rows), f32),
        ),
        in_specs=[by_rows]
        + [unblocked(source) for source in columns]
        + [by_rows, one_row][: len(before)],
        out_specs=(by_rows, one_row),
        compiler_params=vmem_params(24),
        cost_estimate=match_cost(rows, tokens, units),
        name="match",
    )(refs, *columns, *before)


def match_last(refs, columns, before, sums, clients, groups):
    rows, tokens = refs.shape
    by_rows, one_row, two_rows = match_specs(rows, tokens, groups)
    shape = (clients // 2, groups, rows // groups // clients, tokens)
    pieces = pl.BlockSpec((shape[0], 1, shape[2], tokens), lambda j: (0, j, 0, 0))
    halves = jax.ShapeDtypeStruct(shape, bf16)
    return pl.pallas_call(
        match_last_kernel,
        grid=(groups,),
        out_shape=(halves, halves, jax.ShapeDtypeStruct((2, rows), f32)),
        in_specs=[by_rows, unblocked(columns), by_rows, one_row],
        out_specs=(pieces, pieces, two_rows),
        compiler_params=vmem_params(24),
        cost_estimate=match_cost(rows, tokens, columns.shape[1]),
        name="match_last",
    )(refs, columns, before, sums)


def tie_kernel(value, *rest):
    rest[-1][...] = value[...]


def tied(value, *others):
    return pl.pallas_call(
        tie_kernel,
        out_shape=jax.ShapeDtypeStruct(value.shape, value.dtype),
        in_specs=[whole] + [anywhere] * len(others),
        out_specs=whole,
        compiler_params=vmem_params(8),
        name="tied",
    )(value, *others)


def place_kernel(place, *refs):
    *pieces, out, wide, sems = refs
    pieces = pieces[: wide.shape[0]]
    size = wide.shape[1]
    copies = []
    for i, piece in enumerate(pieces):
        at = pl.ds(pl.multiple_of((place[1] ^ i) * size, 8), size)
        wide[i] = piece[...].astype(f32)
        copies.append(pltpu.make_async_copy(wide.at[i], out.at[at, :], sems.at[i]))
        copies[-1].start()
    for copy in copies:
        copy.wait()


def placed(place, pieces, units, after):
    size, tokens = pieces[0].shape
    return pl.pallas_call(
        place_kernel,
        out_shape=jax.ShapeDtypeStruct((units, tokens), f32),
        in_specs=[scalars] + [whole] * len(pieces) + [anywhere] * len(after),
        out_specs=anywhere,
        scratch_shapes=[
            pltpu.VMEM((len(pieces), size, tokens), f32),
            pltpu.SemaphoreType.DMA((len(pieces),)),
        ],
        compiler_params=vmem_params(16),
        cost_estimate=cost(1e5, 6 * units * tokens),
        name="placed",
    )(place, *pieces, *after)


def body(clients, parts, token_ids, embed_table, norm_gain, client_gate, client_up, ref_gate, ref_up):
    client = lax.axis_index("client")
    unit = lax.axis_index("unit")
    place = jnp.stack([client * parts + unit, client]).astype(jnp.int32)
    over_clients = functools.partial(xor_permute, axis="client", size=clients)
    over_units = functools.partial(xor_permute, axis="unit", size=parts)

    def gathered(own, after=()):
        blocks = [own] + [None] * (clients - 1)
        far = tied(own, *after) if after else own
        for p in range(2, clients, 2):
            blocks[p] = over_clients(far, mask=p)
        for p in range(0, clients, 2):
            blocks[p + 1] = over_clients(blocks[p], mask=1)
        return blocks

    def summed_pairs(keep, send):
        return keep.astype(f32) + over_clients(send, mask=1).astype(f32)

    def sent(total):
        return [over_clients(total[p // 2].astype(bf16), mask=p) for p in range(2, clients, 2)]

    def summed(total, arrived):
        mine = total[0]
        for other in arrived:
            mine = mine + other.astype(f32)
        return mine

    keep, send = select_rows(token_ids, place, norm_gain, embed_table, clients)
    total = summed_pairs(keep, send)
    half = total.shape[1] // 2
    halves = [total[:, :half], total[:, half:]]
    halves = [(part, sent(part)) for part in halves]
    halves = [summed(*part).astype(bf16) for part in halves]
    bit = 1
    while bit < parts:
        halves = [part + over_units(part, mask=bit) for part in halves]
        bit *= 2
    own_rows = jnp.concatenate(halves, axis=0)

    ref_keep, ref_send = reference_partials(place, own_rows, ref_gate, ref_up, clients)
    total = summed_pairs(ref_keep, ref_send)
    arrived = sent(total)
    blocks = gathered(own_rows, [total])
    pre = summed(total, arrived)
    ref_piece = standardized(gated(pre[0], pre[1]), 1)
    even = range(0, parts, 2)
    groups, (piece, tokens) = len(even), ref_piece.shape
    ref_pieces = jnp.stack([over_units(ref_piece, mask=k) if k else ref_piece for k in even])
    refs = jnp.stack(gathered(ref_pieces), axis=1).reshape(groups * clients * piece, tokens)

    units = client_gate.shape[2]
    cuts = [0, 3 * units // 7, units]
    own = [
        client_activations(place, blocks, client_gate, client_up, first, last)
        for first, last in zip(cuts, cuts[1:])
    ]
    theirs = [over_units(part, mask=1) for part in own]
    numerator, sums = match(refs, own, groups)
    numerator, sums = match(refs, theirs[:1], groups, (numerator, sums))
    keep, send, sums = match_last(refs, theirs[1], numerator, sums, clients, groups)
    arrived = over_clients(send, mask=1)

    sums = sums.reshape(2, groups, clients * piece)
    all_sums = sums
    for k in even[1:]:
        other = over_units(sums, mask=k)
        all_sums = all_sums + jnp.stack([other[:, g ^ (k // 2)] for g in range(groups)], axis=1)
    colsum, weighted = all_sums[0], all_sums[1]
    factor = (sums[0] * (1.0 / clients) / colsum).reshape(1, groups * clients * piece)
    factor_arrived = over_clients(factor, mask=1)
    reduced = [None] * groups
    after = ()
    for g in reversed(range(groups)):
        first, *others = joined(g, keep, arrived, factor, factor_arrived, after)
        after = others[:1]
        reduced[g] = first
        for p in range(2, clients, 2):
            reduced[g] = reduced[g] + over_clients(others[p // 2 - 1], mask=p).astype(f32)

    score = (weighted[0] / colsum[0]).reshape(clients, piece)
    here = jnp.arange(clients)[:, None] ^ client == jnp.arange(clients)[None, :]
    score = jnp.sum(jnp.where(here[:, :, None], score[None], 0.0), axis=1)
    score = score.reshape(1, clients * piece)

    mine = reduced[0]
    for k in even[1:]:
        mine = mine + over_units(reduced[k // 2].astype(bf16), mask=k).astype(f32)
    pieces = gathered(mine.astype(bf16))
    merged = placed(place, pieces, units, [score])
    return (merged, score)


def solution(mesh):
    in_specs = (
        P(),
        P(("client", "unit"), None),
        P(),
        P("client", None, "unit"),
        P("client", None, "unit"),
        P("client", "unit"),
        P("client", "unit"),
    )
    out_specs = (P("unit", None), P("client", "unit"))
    local = functools.partial(body, mesh.shape["client"], mesh.shape["unit"])
    return jax.shard_map(local, mesh=mesh, in_specs=in_specs, out_specs=out_specs, check_vma=False)
```

```python
import functools

import jax
import jax.numpy as jnp
from jax import lax
from jax.experimental import pallas as pl
from jax.experimental.pallas import tpu as pltpu
from jax.sharding import PartitionSpec as P

sharpness = 40.0
log2_e = 1.4426950408889634
group_rows = 16
fetch_slots = 16
bf16 = jnp.bfloat16
f32 = jnp.float32
whole = pl.BlockSpec(memory_space=pltpu.VMEM)
scalars = pl.BlockSpec(memory_space=pltpu.SMEM)
anywhere = pl.BlockSpec(memory_space=pl.ANY)
in_hbm = pl.BlockSpec(memory_space=pltpu.HBM)


def vmem_params(mib):
    return pltpu.CompilerParams(vmem_limit_bytes=mib * 1024 * 1024)


def cost(flops, bytes_accessed, transcendentals=0):
    return pl.CostEstimate(
        flops=int(flops), bytes_accessed=int(bytes_accessed), transcendentals=int(transcendentals)
    )


def xor_permute(value, axis, size, mask):
    return lax.ppermute(value, axis, [(i, i ^ mask) for i in range(size)])


def select_kernel(place, ids_far, gain_far, table, keep, send, ids, gain, rows, held, slots, sems, first):
    arrivals = [
        pltpu.make_async_copy(ids_far, ids, first.at[0]),
        pltpu.make_async_copy(gain_far, gain, first.at[1]),
    ]
    for arrival in arrivals:
        arrival.start()
    for arrival in arrivals:
        arrival.wait()
    tokens, width = rows.shape
    rows_here = table.shape[0]
    start = place[0] * rows_here
    client = place[1]

    def note(t, count):
        local = ids[t] - start
        held[count] = t
        return count + jnp.logical_and(local >= 0, local < rows_here).astype(jnp.int32)

    def fetch(k):
        t = held[k]
        group = pl.multiple_of((ids[t] - start) // group_rows * group_rows, group_rows)
        slot = lax.rem(k, fetch_slots)
        return pltpu.make_async_copy(
            table.at[pl.ds(group, group_rows), :], slots.at[slot], sems.at[slot]
        )

    count = lax.fori_loop(0, tokens, note, jnp.int32(0), unroll=8)

    def begin(k, carry):
        fetch(k).start()
        return carry

    lax.fori_loop(0, jnp.minimum(count, fetch_slots), begin, 0)
    rows[...] = jnp.zeros_like(rows)
    sublane = lax.broadcasted_iota(jnp.int32, (group_rows, width), 0)

    def place_row(k, carry):
        fetch(k).wait()
        t = held[k]
        row_in_group = lax.rem(ids[t] - start, group_rows)
        block = slots[lax.rem(k, fetch_slots)].astype(f32)
        row = jnp.sum(jnp.where(sublane == row_in_group, block, 0.0), axis=0, keepdims=True)
        scale = lax.rsqrt(jnp.sum(row * row, axis=1, keepdims=True) * (1.0 / width) + 1e-05)
        rows[pl.ds(t, 1), :] = row * scale * gain[...]

        @pl.when(k + fetch_slots < count)
        def _():
            fetch(k + fetch_slots).start()

        return carry

    lax.fori_loop(0, count, place_row, 0)
    span = keep.shape[2]
    for p in range(2 * keep.shape[0]):
        source = pl.multiple_of((client ^ p) * span, span)
        target = send if p % 2 else keep
        target[p // 2] = rows[:, pl.ds(source, span)].astype(bf16)


def select_rows(token_ids, place, norm_gain, embed_table, clients):
    tokens, width = token_ids.shape[0], embed_table.shape[1]
    half = jax.ShapeDtypeStruct((clients // 2, tokens, width // clients), bf16)
    return pl.pallas_call(
        select_kernel,
        out_shape=(half, half),
        in_specs=[scalars, in_hbm, in_hbm, in_hbm],
        out_specs=(whole, whole),
        scratch_shapes=[
            pltpu.SMEM((tokens,), jnp.int32),
            pltpu.VMEM((1, width), f32),
            pltpu.VMEM((tokens, width), f32),
            pltpu.SMEM((tokens + 1,), jnp.int32),
            pltpu.VMEM((fetch_slots, group_rows, width), bf16),
            pltpu.SemaphoreType.DMA((fetch_slots,)),
            pltpu.SemaphoreType.DMA((2,)),
        ],
        compiler_params=vmem_params(48),
        cost_estimate=cost(4e6, 4e6),
        name="select_rows",
    )(place, token_ids, norm_gain[None, :], embed_table)


def standardized(hidden, axis):
    count = hidden.shape[axis]
    center = jnp.sum(hidden, axis=axis, keepdims=True) * (1.0 / count)
    shifted = hidden - center
    spread = jnp.sum(shifted * shifted, axis=axis, keepdims=True) * (1.0 / count)
    return (shifted * lax.rsqrt(spread + 1e-06)).astype(bf16)


def gated(gate, up):
    return gate / (1.0 + jnp.exp(-gate)) * up


def client_kernel(first, place, *refs):
    *blocks, gate_w, up_w, out = refs
    client = place[1]
    tokens, span = blocks[0].shape
    wide = out.shape[1]
    units = pl.ds(pl.multiple_of((first + pl.program_id(0)) * wide, wide), wide)
    gate = jnp.zeros((tokens, wide), f32)
    up = jnp.zeros((tokens, wide), f32)
    for p, block in enumerate(blocks):
        features = pl.ds(pl.multiple_of((client ^ p) * span, span), span)
        gate += jnp.dot(block[...], gate_w[0, features, :], preferred_element_type=f32)
        up += jnp.dot(block[...], up_w[0, features, units], preferred_element_type=f32)
    out[...] = standardized(gated(gate, up), 0)


def client_activations(place, blocks, client_gate, client_up, first, last):
    tokens = blocks[0].shape[0]
    width, units = client_gate.shape[1], last - first
    wide = unit_block(client_gate.shape[2])
    start = first // wide
    return pl.pallas_call(
        functools.partial(client_kernel, start),
        grid=(units // wide,),
        out_shape=jax.ShapeDtypeStruct((tokens, units), bf16),
        in_specs=[scalars]
        + [whole] * len(blocks)
        + [pl.BlockSpec((1, width, wide), lambda i: (0, 0, start + i)), whole],
        out_specs=pl.BlockSpec((tokens, wide), lambda i: (0, i)),
        compiler_params=vmem_params(12),
        cost_estimate=cost(4 * tokens * width * units, 4 * width * units),
        name="client_activations",
    )(place, *blocks, client_gate, client_up)


def unit_block(units, most=256):
    return most if units % most == 0 else most // 2


def partial_kernel(place, rows, gate_w, up_w, keep, send, total):
    wide = unit_block(gate_w.shape[1])
    for which, weights in enumerate((gate_w, up_w)):
        for at in range(0, weights.shape[1], wide):
            total[which, at : at + wide, :] = lax.dot_general(
                weights[:, at : at + wide],
                rows[...],
                (((0,), (1,)), ((), ())),
                preferred_element_type=f32,
            )
    piece = keep.shape[2]
    for p in range(2 * keep.shape[0]):
        source = pl.ds(pl.multiple_of((place[1] ^ p) * piece, 8), piece)
        for which in range(2):
            if p % 2:
                send[p // 2, which] = total[which, source, :].astype(bf16)
            else:
                keep[p // 2, which] = total[which, source, :]


def reference_partials(place, rows, ref_gate, ref_up, clients):
    tokens, span = rows.shape
    units = ref_gate.shape[1]
    shape = (clients // 2, 2, units // clients, tokens)
    return pl.pallas_call(
        partial_kernel,
        out_shape=(jax.ShapeDtypeStruct(shape, f32), jax.ShapeDtypeStruct(shape, bf16)),
        in_specs=[scalars] + [whole] * 3,
        out_specs=(whole, whole),
        scratch_shapes=[pltpu.VMEM((2, units, tokens), f32)],
        compiler_params=vmem_params(16),
        cost_estimate=cost(4 * tokens * span * units, 4 * span * units),
        name="reference_partials",
    )(place, rows, ref_gate, ref_up)


def matched(rows, columns, total):
    tokens = rows.shape[1]
    colsum = jnp.zeros((rows.shape[0], 128), f32)
    for source in columns:
        wide = unit_block(source.shape[1])
        for i in range(0, source.shape[1], wide):
            some = source[:, i : i + wide]
            r = jnp.dot(rows, some, preferred_element_type=f32)
            w = jnp.exp2(r * (sharpness * log2_e / tokens))
            total += lax.dot_general(
                w.astype(bf16), some, (((1,), (1,)), ((), ())), preferred_element_type=f32
            )
            for k in range(0, wide, 128):
                colsum += w[:, k : k + 128]
    return total, jnp.sum(colsum.T, axis=0, keepdims=True)


def match_kernel(sources, refs, *rest):
    columns, rest = rest[:sources], rest[sources:]
    numerator, sums = rest[-2:]
    before = rest[:-2]
    start = before[0][...] if before else jnp.zeros(numerator.shape, f32)
    numerator[...], row = matched(refs[...], columns, start)
    sums[...] = row + before[1][...] if before else row


def match_last_kernel(refs, columns, before, sums_before, keep, send, sums):
    total, row = matched(refs[...], [columns], before[...])
    tokens, lanes = total.shape[1], 128
    row = row + sums_before[...]
    sums[0:1, :] = row
    weighted = total * refs[...].astype(f32)
    weighted = sum(weighted[:, k : k + lanes] for k in range(0, tokens, lanes))
    sums[1:2, :] = jnp.sum(weighted.T, axis=0, keepdims=True) * (1.0 / tokens)
    by_row = jnp.broadcast_to(1.0 / row, (lanes, total.shape[0])).T
    size = keep.shape[2]
    for p in range(2 * keep.shape[0]):
        target = send if p % 2 else keep
        units = slice(p * size, (p + 1) * size)
        for k in range(0, tokens, lanes):
            target[p // 2, 0, :, k : k + lanes] = (total[units, k : k + lanes] * by_row[units]).astype(
                target.dtype
            )


def join_kernel(group, keep, arrived, factor, factor_arrived, *refs):
    pairs, _, size, tokens = keep.shape
    first, *others = refs[-pairs:]
    lanes = 128
    units = 2 * pairs * size
    rows = [
        jnp.broadcast_to(source[:, group * units : (group + 1) * units], (lanes, units)).T
        for source in (factor, factor_arrived)
    ]
    for h in range(pairs):
        ours = slice(2 * h * size, (2 * h + 1) * size)
        theirs = slice((2 * h + 1) * size, (2 * h + 2) * size)
        for k in range(0, tokens, lanes):
            at = slice(k, k + lanes)
            total = keep[h, group, :, at].astype(f32) * rows[0][ours]
            total += arrived[h, group, :, at].astype(f32) * rows[1][theirs]
            if h:
                others[h - 1][:, at] = total.astype(bf16)
            else:
                first[:, at] = total


def joined(group, keep, arrived, factor, factor_arrived, after):
    pairs, _, size, tokens = keep.shape
    piece = jax.ShapeDtypeStruct((size, tokens), bf16)
    return pl.pallas_call(
        functools.partial(join_kernel, group),
        out_shape=(jax.ShapeDtypeStruct((size, tokens), f32), *[piece] * (pairs - 1)),
        in_specs=[whole] * 4 + [anywhere] * len(after),
        out_specs=(whole,) * pairs,
        compiler_params=vmem_params(16),
        cost_estimate=cost(4 * pairs * size * tokens, 6 * pairs * size * tokens),
        name="joined",
    )(keep, arrived, factor, factor_arrived, *after)


def match_cost(rows, tokens, units):
    return cost(4 * rows * units * tokens, 8 * rows * tokens, rows * units)


def match_specs(rows, tokens, groups):
    high = rows // groups
    by_rows = pl.BlockSpec((high, tokens), lambda j: (j, 0))
    return by_rows, *[pl.BlockSpec((n, high), lambda j: (0, j)) for n in (1, 2)]


def unblocked(value):
    return pl.BlockSpec(value.shape, lambda j: (0, 0))


def match(refs, columns, groups, before=()):
    rows, tokens = refs.shape
    units = sum(source.shape[1] for source in columns)
    by_rows, one_row, _ = match_specs(rows, tokens, groups)
    return pl.pallas_call(
        functools.partial(match_kernel, len(columns)),
        grid=(groups,),
        out_shape=(
            jax.ShapeDtypeStruct((rows, tokens), f32),
            jax.ShapeDtypeStruct((1, rows), f32),
        ),
        in_specs=[by_rows]
        + [unblocked(source) for source in columns]
        + [by_rows, one_row][: len(before)],
        out_specs=(by_rows, one_row),
        compiler_params=vmem_params(24),
        cost_estimate=match_cost(rows, tokens, units),
        name="match",
    )(refs, *columns, *before)


def match_last(refs, columns, before, sums, clients, groups):
    rows, tokens = refs.shape
    by_rows, one_row, two_rows = match_specs(rows, tokens, groups)
    shape = (clients // 2, groups, rows // groups // clients, tokens)
    pieces = pl.BlockSpec((shape[0], 1, shape[2], tokens), lambda j: (0, j, 0, 0))
    halves = jax.ShapeDtypeStruct(shape, bf16)
    return pl.pallas_call(
        match_last_kernel,
        grid=(groups,),
        out_shape=(halves, halves, jax.ShapeDtypeStruct((2, rows), f32)),
        in_specs=[by_rows, unblocked(columns), by_rows, one_row],
        out_specs=(pieces, pieces, two_rows),
        compiler_params=vmem_params(24),
        cost_estimate=match_cost(rows, tokens, columns.shape[1]),
        name="match_last",
    )(refs, columns, before, sums)


def tie_kernel(value, *rest):
    rest[-1][...] = value[...]


def tied(value, *others):
    return pl.pallas_call(
        tie_kernel,
        out_shape=jax.ShapeDtypeStruct(value.shape, value.dtype),
        in_specs=[whole] + [anywhere] * len(others),
        out_specs=whole,
        compiler_params=vmem_params(8),
        name="tied",
    )(value, *others)


def place_kernel(place, *refs):
    *pieces, out, wide, sems = refs
    pieces = pieces[: wide.shape[0]]
    size = wide.shape[1]
    copies = []
    for i, piece in enumerate(pieces):
        at = pl.ds(pl.multiple_of((place[1] ^ i) * size, 8), size)
        wide[i] = piece[...].astype(f32)
        copies.append(pltpu.make_async_copy(wide.at[i], out.at[at, :], sems.at[i]))
        copies[-1].start()
    for copy in copies:
        copy.wait()


def placed(place, pieces, units, after):
    size, tokens = pieces[0].shape
    return pl.pallas_call(
        place_kernel,
        out_shape=jax.ShapeDtypeStruct((units, tokens), f32),
        in_specs=[scalars] + [whole] * len(pieces) + [anywhere] * len(after),
        out_specs=anywhere,
        scratch_shapes=[
            pltpu.VMEM((len(pieces), size, tokens), f32),
            pltpu.SemaphoreType.DMA((len(pieces),)),
        ],
        compiler_params=vmem_params(16),
        cost_estimate=cost(1e5, 6 * units * tokens),
        name="placed",
    )(place, *pieces, *after)


def body(clients, parts, token_ids, embed_table, norm_gain, client_gate, client_up, ref_gate, ref_up):
    client = lax.axis_index("client")
    unit = lax.axis_index("unit")
    place = jnp.stack([client * parts + unit, client]).astype(jnp.int32)
    over_clients = functools.partial(xor_permute, axis="client", size=clients)
    over_units = functools.partial(xor_permute, axis="unit", size=parts)

    def gathered(own, after=()):
        blocks = [own] + [None] * (clients - 1)
        far = tied(own, *after) if after else own
        for p in range(2, clients, 2):
            blocks[p] = over_clients(far, mask=p)
        for p in range(0, clients, 2):
            blocks[p + 1] = over_clients(blocks[p], mask=1)
        return blocks

    def summed_pairs(keep, send):
        return keep.astype(f32) + over_clients(send, mask=1).astype(f32)

    def sent(total):
        return [over_clients(total[p // 2].astype(bf16), mask=p) for p in range(2, clients, 2)]

    def summed(total, arrived):
        mine = total[0]
        for other in arrived:
            mine = mine + other.astype(f32)
        return mine

    keep, send = select_rows(token_ids, place, norm_gain, embed_table, clients)
    total = summed_pairs(keep, send)
    half = total.shape[1] // 2
    halves = [total[:, :half], total[:, half:]]
    halves = [(part, sent(part)) for part in halves]
    early, late = halves
    early = summed(*early).astype(bf16)
    met = over_units(early, mask=1)
    late = summed([tied(late[0][0], met)], late[1]).astype(bf16)
    halves = [early + met, late + over_units(late, mask=1)]
    bit = 2
    while bit < parts:
        halves = [part + over_units(part, mask=bit) for part in halves]
        bit *= 2
    own_rows = jnp.concatenate(halves, axis=0)

    ref_keep, ref_send = reference_partials(place, own_rows, ref_gate, ref_up, clients)
    total = summed_pairs(ref_keep, ref_send)
    arrived = sent(total)
    blocks = gathered(own_rows, [total])
    pre = summed(total, arrived)
    ref_piece = standardized(gated(pre[0], pre[1]), 1)
    even = range(0, parts, 2)
    groups, (piece, tokens) = len(even), ref_piece.shape
    ref_pieces = jnp.stack([over_units(ref_piece, mask=k) if k else ref_piece for k in even])
    refs = jnp.stack(gathered(ref_pieces), axis=1).reshape(groups * clients * piece, tokens)

    units = client_gate.shape[2]
    cuts = [0, 3 * units // 7, units]
    own = [
        client_activations(place, blocks, client_gate, client_up, first, last)
        for first, last in zip(cuts, cuts[1:])
    ]
    theirs = [over_units(part, mask=1) for part in own]
    numerator, sums = match(refs, own, groups)
    numerator, sums = match(refs, theirs[:1], groups, (numerator, sums))
    keep, send, sums = match_last(refs, theirs[1], numerator, sums, clients, groups)
    arrived = over_clients(send, mask=1)

    sums = sums.reshape(2, groups, clients * piece)
    all_sums = sums
    for k in even[1:]:
        other = over_units(sums, mask=k)
        all_sums = all_sums + jnp.stack([other[:, g ^ (k // 2)] for g in range(groups)], axis=1)
    colsum, weighted = all_sums[0], all_sums[1]
    factor = (sums[0] * (1.0 / clients) / colsum).reshape(1, groups * clients * piece)
    factor_arrived = over_clients(factor, mask=1)
    reduced = [None] * groups
    after = ()
    for g in reversed(range(groups)):
        first, *others = joined(g, keep, arrived, factor, factor_arrived, after)
        after = others[:1]
        reduced[g] = first
        for p in range(2, clients, 2):
            reduced[g] = reduced[g] + over_clients(others[p // 2 - 1], mask=p).astype(f32)

    score = (weighted[0] / colsum[0]).reshape(clients, piece)
    here = jnp.arange(clients)[:, None] ^ client == jnp.arange(clients)[None, :]
    score = jnp.sum(jnp.where(here[:, :, None], score[None], 0.0), axis=1)
    score = score.reshape(1, clients * piece)

    mine = reduced[0]
    for k in even[1:]:
        mine = mine + over_units(reduced[k // 2].astype(bf16), mask=k).astype(f32)
    pieces = gathered(mine.astype(bf16))
    merged = placed(place, pieces, units, [score])
    return (merged, score)


def solution(mesh):
    in_specs = (
        P(),
        P(("client", "unit"), None),
        P(),
        P("client", None, "unit"),
        P("client", None, "unit"),
        P("client", "unit"),
        P("client", "unit"),
    )
    out_specs = (P("unit", None), P("client", "unit"))
    local = functools.partial(body, mesh.shape["client"], mesh.shape["unit"])
    return jax.shard_map(local, mesh=mesh, in_specs=in_specs, out_specs=out_specs, check_vma=False)
```

```python
import functools

import jax
import jax.numpy as jnp
from jax import lax
from jax.experimental import pallas as pl
from jax.experimental.pallas import tpu as pltpu
from jax.sharding import PartitionSpec as P

sharpness = 40.0
log2_e = 1.4426950408889634
group_rows = 16
fetch_slots = 16
bf16 = jnp.bfloat16
f32 = jnp.float32
whole = pl.BlockSpec(memory_space=pltpu.VMEM)
scalars = pl.BlockSpec(memory_space=pltpu.SMEM)
anywhere = pl.BlockSpec(memory_space=pl.ANY)
in_hbm = pl.BlockSpec(memory_space=pltpu.HBM)


def vmem_params(mib):
    return pltpu.CompilerParams(vmem_limit_bytes=mib * 1024 * 1024)


def cost(flops, bytes_accessed, transcendentals=0):
    return pl.CostEstimate(
        flops=int(flops), bytes_accessed=int(bytes_accessed), transcendentals=int(transcendentals)
    )


def xor_permute(value, axis, size, mask):
    return lax.ppermute(value, axis, [(i, i ^ mask) for i in range(size)])


def select_kernel(place, ids_far, gain_far, table, keep, send, ids, gain, rows, held, slots, sems, first):
    arrivals = [
        pltpu.make_async_copy(ids_far, ids, first.at[0]),
        pltpu.make_async_copy(gain_far, gain, first.at[1]),
    ]
    for arrival in arrivals:
        arrival.start()
    for arrival in arrivals:
        arrival.wait()
    tokens, width = rows.shape
    rows_here = table.shape[0]
    start = place[0] * rows_here
    client = place[1]

    def note(t, count):
        local = ids[t] - start
        held[count] = t
        return count + jnp.logical_and(local >= 0, local < rows_here).astype(jnp.int32)

    def fetch(k):
        t = held[k]
        group = pl.multiple_of((ids[t] - start) // group_rows * group_rows, group_rows)
        slot = lax.rem(k, fetch_slots)
        return pltpu.make_async_copy(
            table.at[pl.ds(group, group_rows), :], slots.at[slot], sems.at[slot]
        )

    count = lax.fori_loop(0, tokens, note, jnp.int32(0), unroll=8)

    def begin(k, carry):
        fetch(k).start()
        return carry

    lax.fori_loop(0, jnp.minimum(count, fetch_slots), begin, 0)
    rows[...] = jnp.zeros_like(rows)
    sublane = lax.broadcasted_iota(jnp.int32, (group_rows, width), 0)

    def place_row(k, carry):
        fetch(k).wait()
        t = held[k]
        row_in_group = lax.rem(ids[t] - start, group_rows)
        block = slots[lax.rem(k, fetch_slots)].astype(f32)
        row = jnp.sum(jnp.where(sublane == row_in_group, block, 0.0), axis=0, keepdims=True)
        rows[pl.ds(t, 1), :] = row

        @pl.when(k + fetch_slots < count)
        def _():
            fetch(k + fetch_slots).start()

        return carry

    lax.fori_loop(0, count, place_row, 0)
    lanes = 128
    squares = jnp.zeros((tokens, lanes), f32)
    for k in range(0, width, lanes):
        some = rows[:, k : k + lanes]
        squares += some * some
    scale = lax.rsqrt(jnp.sum(squares, axis=1, keepdims=True) * (1.0 / width) + 1e-05)
    span = keep.shape[2]
    for p in range(2 * keep.shape[0]):
        source = pl.ds(pl.multiple_of((client ^ p) * span, span), span)
        target = send if p % 2 else keep
        target[p // 2] = (rows[:, source] * scale * gain[:, source]).astype(bf16)


def select_rows(token_ids, place, norm_gain, embed_table, clients):
    tokens, width = token_ids.shape[0], embed_table.shape[1]
    half = jax.ShapeDtypeStruct((clients // 2, tokens, width // clients), bf16)
    return pl.pallas_call(
        select_kernel,
        out_shape=(half, half),
        in_specs=[scalars, in_hbm, in_hbm, in_hbm],
        out_specs=(whole, whole),
        scratch_shapes=[
            pltpu.SMEM((tokens,), jnp.int32),
            pltpu.VMEM((1, width), f32),
            pltpu.VMEM((tokens, width), f32),
            pltpu.SMEM((tokens + 1,), jnp.int32),
            pltpu.VMEM((fetch_slots, group_rows, width), bf16),
            pltpu.SemaphoreType.DMA((fetch_slots,)),
            pltpu.SemaphoreType.DMA((2,)),
        ],
        compiler_params=vmem_params(48),
        cost_estimate=cost(4e6, 4e6),
        name="select_rows",
    )(place, token_ids, norm_gain[None, :], embed_table)


def standardized(hidden, axis):
    count = hidden.shape[axis]
    center = jnp.sum(hidden, axis=axis, keepdims=True) * (1.0 / count)
    shifted = hidden - center
    spread = jnp.sum(shifted * shifted, axis=axis, keepdims=True) * (1.0 / count)
    return (shifted * lax.rsqrt(spread + 1e-06)).astype(bf16)


def gated(gate, up):
    return gate / (1.0 + jnp.exp(-gate)) * up


def client_kernel(first, place, *refs):
    *blocks, gate_w, up_w, out = refs
    client = place[1]
    tokens, span = blocks[0].shape
    wide = out.shape[1]
    units = pl.ds(pl.multiple_of((first + pl.program_id(0)) * wide, wide), wide)
    gate = jnp.zeros((tokens, wide), f32)
    up = jnp.zeros((tokens, wide), f32)
    for p, block in enumerate(blocks):
        features = pl.ds(pl.multiple_of((client ^ p) * span, span), span)
        gate += jnp.dot(block[...], gate_w[0, features, :], preferred_element_type=f32)
        up += jnp.dot(block[...], up_w[0, features, units], preferred_element_type=f32)
    out[...] = standardized(gated(gate, up), 0)


def client_activations(place, blocks, client_gate, client_up, first, last):
    tokens = blocks[0].shape[0]
    width, units = client_gate.shape[1], last - first
    wide = unit_block(client_gate.shape[2])
    start = first // wide
    return pl.pallas_call(
        functools.partial(client_kernel, start),
        grid=(units // wide,),
        out_shape=jax.ShapeDtypeStruct((tokens, units), bf16),
        in_specs=[scalars]
        + [whole] * len(blocks)
        + [pl.BlockSpec((1, width, wide), lambda i: (0, 0, start + i)), whole],
        out_specs=pl.BlockSpec((tokens, wide), lambda i: (0, i)),
        compiler_params=vmem_params(12),
        cost_estimate=cost(4 * tokens * width * units, 4 * width * units),
        name="client_activations",
    )(place, *blocks, client_gate, client_up)


def unit_block(units, most=256):
    return most if units % most == 0 else most // 2


def partial_kernel(place, rows, gate_w, up_w, keep, send, total):
    wide = unit_block(gate_w.shape[1])
    for which, weights in enumerate((gate_w, up_w)):
        for at in range(0, weights.shape[1], wide):
            total[which, at : at + wide, :] = lax.dot_general(
                weights[:, at : at + wide],
                rows[...],
                (((0,), (1,)), ((), ())),
                preferred_element_type=f32,
            )
    piece = keep.shape[2]
    for p in range(2 * keep.shape[0]):
        source = pl.ds(pl.multiple_of((place[1] ^ p) * piece, 8), piece)
        for which in range(2):
            if p % 2:
                send[p // 2, which] = total[which, source, :].astype(bf16)
            else:
                keep[p // 2, which] = total[which, source, :]


def reference_partials(place, rows, ref_gate, ref_up, clients):
    tokens, span = rows.shape
    units = ref_gate.shape[1]
    shape = (clients // 2, 2, units // clients, tokens)
    return pl.pallas_call(
        partial_kernel,
        out_shape=(jax.ShapeDtypeStruct(shape, f32), jax.ShapeDtypeStruct(shape, bf16)),
        in_specs=[scalars] + [whole] * 3,
        out_specs=(whole, whole),
        scratch_shapes=[pltpu.VMEM((2, units, tokens), f32)],
        compiler_params=vmem_params(16),
        cost_estimate=cost(4 * tokens * span * units, 4 * span * units),
        name="reference_partials",
    )(place, rows, ref_gate, ref_up)


def matched(rows, columns, total):
    tokens = rows.shape[1]
    colsum = jnp.zeros((rows.shape[0], 128), f32)
    for source in columns:
        wide = unit_block(source.shape[1])
        for i in range(0, source.shape[1], wide):
            some = source[:, i : i + wide]
            r = jnp.dot(rows, some, preferred_element_type=f32)
            w = jnp.exp2(r * (sharpness * log2_e / tokens))
            total += lax.dot_general(
                w.astype(bf16), some, (((1,), (1,)), ((), ())), preferred_element_type=f32
            )
            for k in range(0, wide, 128):
                colsum += w[:, k : k + 128]
    return total, jnp.sum(colsum.T, axis=0, keepdims=True)


def match_kernel(sources, refs, *rest):
    columns, rest = rest[:sources], rest[sources:]
    numerator, sums = rest[-2:]
    before = rest[:-2]
    start = before[0][...] if before else jnp.zeros(numerator.shape, f32)
    numerator[...], row = matched(refs[...], columns, start)
    sums[...] = row + before[1][...] if before else row


def match_last_kernel(refs, columns, before, sums_before, keep, send, sums):
    total, row = matched(refs[...], [columns], before[...])
    tokens, lanes = total.shape[1], 128
    row = row + sums_before[...]
    sums[0:1, :] = row
    weighted = total * refs[...].astype(f32)
    weighted = sum(weighted[:, k : k + lanes] for k in range(0, tokens, lanes))
    sums[1:2, :] = jnp.sum(weighted.T, axis=0, keepdims=True) * (1.0 / tokens)
    by_row = jnp.broadcast_to(1.0 / row, (lanes, total.shape[0])).T
    size = keep.shape[2]
    for p in range(2 * keep.shape[0]):
        target = send if p % 2 else keep
        units = slice(p * size, (p + 1) * size)
        for k in range(0, tokens, lanes):
            target[p // 2, 0, :, k : k + lanes] = (total[units, k : k + lanes] * by_row[units]).astype(
                target.dtype
            )


def join_kernel(group, keep, arrived, factor, factor_arrived, *refs):
    pairs, _, size, tokens = keep.shape
    first, *others = refs[-pairs:]
    lanes = 128
    units = 2 * pairs * size
    rows = [
        jnp.broadcast_to(source[:, group * units : (group + 1) * units], (lanes, units)).T
        for source in (factor, factor_arrived)
    ]
    for h in range(pairs):
        ours = slice(2 * h * size, (2 * h + 1) * size)
        theirs = slice((2 * h + 1) * size, (2 * h + 2) * size)
        for k in range(0, tokens, lanes):
            at = slice(k, k + lanes)
            total = keep[h, group, :, at].astype(f32) * rows[0][ours]
            total += arrived[h, group, :, at].astype(f32) * rows[1][theirs]
            if h:
                others[h - 1][:, at] = total.astype(bf16)
            else:
                first[:, at] = total


def joined(group, keep, arrived, factor, factor_arrived, after):
    pairs, _, size, tokens = keep.shape
    piece = jax.ShapeDtypeStruct((size, tokens), bf16)
    return pl.pallas_call(
        functools.partial(join_kernel, group),
        out_shape=(jax.ShapeDtypeStruct((size, tokens), f32), *[piece] * (pairs - 1)),
        in_specs=[whole] * 4 + [anywhere] * len(after),
        out_specs=(whole,) * pairs,
        compiler_params=vmem_params(16),
        cost_estimate=cost(4 * pairs * size * tokens, 6 * pairs * size * tokens),
        name="joined",
    )(keep, arrived, factor, factor_arrived, *after)


def match_cost(rows, tokens, units):
    return cost(4 * rows * units * tokens, 8 * rows * tokens, rows * units)


def match_specs(rows, tokens, groups):
    high = rows // groups
    by_rows = pl.BlockSpec((high, tokens), lambda j: (j, 0))
    return by_rows, *[pl.BlockSpec((n, high), lambda j: (0, j)) for n in (1, 2)]


def unblocked(value):
    return pl.BlockSpec(value.shape, lambda j: (0, 0))


def match(refs, columns, groups, before=()):
    rows, tokens = refs.shape
    units = sum(source.shape[1] for source in columns)
    by_rows, one_row, _ = match_specs(rows, tokens, groups)
    return pl.pallas_call(
        functools.partial(match_kernel, len(columns)),
        grid=(groups,),
        out_shape=(
            jax.ShapeDtypeStruct((rows, tokens), f32),
            jax.ShapeDtypeStruct((1, rows), f32),
        ),
        in_specs=[by_rows]
        + [unblocked(source) for source in columns]
        + [by_rows, one_row][: len(before)],
        out_specs=(by_rows, one_row),
        compiler_params=vmem_params(24),
        cost_estimate=match_cost(rows, tokens, units),
        name="match",
    )(refs, *columns, *before)


def match_last(refs, columns, before, sums, clients, groups):
    rows, tokens = refs.shape
    by_rows, one_row, two_rows = match_specs(rows, tokens, groups)
    shape = (clients // 2, groups, rows // groups // clients, tokens)
    pieces = pl.BlockSpec((shape[0], 1, shape[2], tokens), lambda j: (0, j, 0, 0))
    halves = jax.ShapeDtypeStruct(shape, bf16)
    return pl.pallas_call(
        match_last_kernel,
        grid=(groups,),
        out_shape=(halves, halves, jax.ShapeDtypeStruct((2, rows), f32)),
        in_specs=[by_rows, unblocked(columns), by_rows, one_row],
        out_specs=(pieces, pieces, two_rows),
        compiler_params=vmem_params(24),
        cost_estimate=match_cost(rows, tokens, columns.shape[1]),
        name="match_last",
    )(refs, columns, before, sums)


def tie_kernel(value, *rest):
    rest[-1][...] = value[...]


def tied(value, *others):
    return pl.pallas_call(
        tie_kernel,
        out_shape=jax.ShapeDtypeStruct(value.shape, value.dtype),
        in_specs=[whole] + [anywhere] * len(others),
        out_specs=whole,
        compiler_params=vmem_params(8),
        name="tied",
    )(value, *others)


def place_kernel(place, *refs):
    *pieces, out, wide, sems = refs
    pieces = pieces[: wide.shape[0]]
    size = wide.shape[1]
    copies = []
    for i, piece in enumerate(pieces):
        at = pl.ds(pl.multiple_of((place[1] ^ i) * size, 8), size)
        wide[i] = piece[...].astype(f32)
        copies.append(pltpu.make_async_copy(wide.at[i], out.at[at, :], sems.at[i]))
        copies[-1].start()
    for copy in copies:
        copy.wait()


def placed(place, pieces, units, after):
    size, tokens = pieces[0].shape
    return pl.pallas_call(
        place_kernel,
        out_shape=jax.ShapeDtypeStruct((units, tokens), f32),
        in_specs=[scalars] + [whole] * len(pieces) + [anywhere] * len(after),
        out_specs=anywhere,
        scratch_shapes=[
            pltpu.VMEM((len(pieces), size, tokens), f32),
            pltpu.SemaphoreType.DMA((len(pieces),)),
        ],
        compiler_params=vmem_params(16),
        cost_estimate=cost(1e5, 6 * units * tokens),
        name="placed",
    )(place, *pieces, *after)


def body(clients, parts, token_ids, embed_table, norm_gain, client_gate, client_up, ref_gate, ref_up):
    client = lax.axis_index("client")
    unit = lax.axis_index("unit")
    place = jnp.stack([client * parts + unit, client]).astype(jnp.int32)
    over_clients = functools.partial(xor_permute, axis="client", size=clients)
    over_units = functools.partial(xor_permute, axis="unit", size=parts)

    def gathered(own, after=()):
        blocks = [own] + [None] * (clients - 1)
        far = tied(own, *after) if after else own
        for p in range(2, clients, 2):
            blocks[p] = over_clients(far, mask=p)
        for p in range(0, clients, 2):
            blocks[p + 1] = over_clients(blocks[p], mask=1)
        return blocks

    def summed_pairs(keep, send):
        return keep.astype(f32) + over_clients(send, mask=1).astype(f32)

    def sent(total):
        return [over_clients(total[p // 2].astype(bf16), mask=p) for p in range(2, clients, 2)]

    def summed(total, arrived):
        mine = total[0]
        for other in arrived:
            mine = mine + other.astype(f32)
        return mine

    keep, send = select_rows(token_ids, place, norm_gain, embed_table, clients)
    total = summed_pairs(keep, send)
    half = total.shape[1] // 2
    halves = [total[:, :half], total[:, half:]]
    halves = [(part, sent(part)) for part in halves]
    early, late = halves
    early = summed(*early).astype(bf16)
    met = over_units(early, mask=1)
    late = summed([tied(late[0][0], met)], late[1]).astype(bf16)
    halves = [early + met, late + over_units(late, mask=1)]
    bit = 2
    while bit < parts:
        halves = [part + over_units(part, mask=bit) for part in halves]
        bit *= 2
    own_rows = jnp.concatenate(halves, axis=0)

    ref_keep, ref_send = reference_partials(place, own_rows, ref_gate, ref_up, clients)
    total = summed_pairs(ref_keep, ref_send)
    arrived = sent(total)
    blocks = gathered(own_rows, [total])
    pre = summed(total, arrived)
    ref_piece = standardized(gated(pre[0], pre[1]), 1)
    even = range(0, parts, 2)
    groups, (piece, tokens) = len(even), ref_piece.shape
    ref_pieces = jnp.stack([over_units(ref_piece, mask=k) if k else ref_piece for k in even])
    refs = jnp.stack(gathered(ref_pieces), axis=1).reshape(groups * clients * piece, tokens)

    units = client_gate.shape[2]
    cuts = [0, 3 * units // 7, units]
    own = [
        client_activations(place, blocks, client_gate, client_up, first, last)
        for first, last in zip(cuts, cuts[1:])
    ]
    theirs = [over_units(part, mask=1) for part in own]
    numerator, sums = match(refs, own, groups)
    numerator, sums = match(refs, theirs[:1], groups, (numerator, sums))
    keep, send, sums = match_last(refs, theirs[1], numerator, sums, clients, groups)
    arrived = over_clients(send, mask=1)

    sums = sums.reshape(2, groups, clients * piece)
    all_sums = sums
    for k in even[1:]:
        other = over_units(sums, mask=k)
        all_sums = all_sums + jnp.stack([other[:, g ^ (k // 2)] for g in range(groups)], axis=1)
    colsum, weighted = all_sums[0], all_sums[1]
    factor = (sums[0] * (1.0 / clients) / colsum).reshape(1, groups * clients * piece)
    factor_arrived = over_clients(factor, mask=1)
    reduced = [None] * groups
    after = ()
    for g in reversed(range(groups)):
        first, *others = joined(g, keep, arrived, factor, factor_arrived, after)
        after = others[:1]
        reduced[g] = first
        for p in range(2, clients, 2):
            reduced[g] = reduced[g] + over_clients(others[p // 2 - 1], mask=p).astype(f32)

    score = (weighted[0] / colsum[0]).reshape(clients, piece)
    here = jnp.arange(clients)[:, None] ^ client == jnp.arange(clients)[None, :]
    score = jnp.sum(jnp.where(here[:, :, None], score[None], 0.0), axis=1)
    score = score.reshape(1, clients * piece)

    mine = reduced[0]
    for k in even[1:]:
        mine = mine + over_units(reduced[k // 2].astype(bf16), mask=k).astype(f32)
    pieces = gathered(mine.astype(bf16))
    merged = placed(place, pieces, units, [score])
    return (merged, score)


def solution(mesh):
    in_specs = (
        P(),
        P(("client", "unit"), None),
        P(),
        P("client", None, "unit"),
        P("client", None, "unit"),
        P("client", "unit"),
        P("client", "unit"),
    )
    out_specs = (P("unit", None), P("client", "unit"))
    local = functools.partial(body, mesh.shape["client"], mesh.shape["unit"])
    return jax.shard_map(local, mesh=mesh, in_specs=in_specs, out_specs=out_specs, check_vma=False)
```

```python
import functools

import jax
import jax.numpy as jnp
from jax import lax
from jax.experimental import pallas as pl
from jax.experimental.pallas import tpu as pltpu
from jax.sharding import PartitionSpec as P

sharpness = 40.0
log2_e = 1.4426950408889634
group_rows = 16
fetch_slots = 32
bf16 = jnp.bfloat16
f32 = jnp.float32
whole = pl.BlockSpec(memory_space=pltpu.VMEM)
scalars = pl.BlockSpec(memory_space=pltpu.SMEM)
anywhere = pl.BlockSpec(memory_space=pl.ANY)
in_hbm = pl.BlockSpec(memory_space=pltpu.HBM)


def vmem_params(mib):
    return pltpu.CompilerParams(vmem_limit_bytes=mib * 1024 * 1024)


def cost(flops, bytes_accessed, transcendentals=0):
    return pl.CostEstimate(
        flops=int(flops), bytes_accessed=int(bytes_accessed), transcendentals=int(transcendentals)
    )


def xor_permute(value, axis, size, mask):
    return lax.ppermute(value, axis, [(i, i ^ mask) for i in range(size)])


def select_kernel(place, ids_far, gain_far, table, keep, send, ids, gain, rows, held, slots, sems, first):
    arrivals = [
        pltpu.make_async_copy(ids_far, ids, first.at[0]),
        pltpu.make_async_copy(gain_far, gain, first.at[1]),
    ]
    for arrival in arrivals:
        arrival.start()
    for arrival in arrivals:
        arrival.wait()
    tokens, width = rows.shape
    rows_here = table.shape[0]
    start = place[0] * rows_here
    client = place[1]

    def note(t, count):
        local = ids[t] - start
        held[count] = t
        return count + jnp.logical_and(local >= 0, local < rows_here).astype(jnp.int32)

    def fetch(k):
        t = held[k]
        group = pl.multiple_of((ids[t] - start) // group_rows * group_rows, group_rows)
        slot = lax.rem(k, fetch_slots)
        return pltpu.make_async_copy(
            table.at[pl.ds(group, group_rows), :], slots.at[slot], sems.at[slot]
        )

    count = lax.fori_loop(0, tokens, note, jnp.int32(0), unroll=8)

    def begin(k, carry):
        fetch(k).start()
        return carry

    lax.fori_loop(0, jnp.minimum(count, fetch_slots), begin, 0)
    rows[...] = jnp.zeros_like(rows)
    sublane = lax.broadcasted_iota(jnp.int32, (group_rows, width), 0)

    def place_row(k, carry):
        fetch(k).wait()
        t = held[k]
        row_in_group = lax.rem(ids[t] - start, group_rows)
        block = slots[lax.rem(k, fetch_slots)].astype(f32)
        row = jnp.sum(jnp.where(sublane == row_in_group, block, 0.0), axis=0, keepdims=True)
        rows[pl.ds(t, 1), :] = row

        @pl.when(k + fetch_slots < count)
        def _():
            fetch(k + fetch_slots).start()

        return carry

    lax.fori_loop(0, count, place_row, 0)
    lanes = 128
    squares = jnp.zeros((tokens, lanes), f32)
    for k in range(0, width, lanes):
        some = rows[:, k : k + lanes]
        squares += some * some
    scale = lax.rsqrt(jnp.sum(squares, axis=1, keepdims=True) * (1.0 / width) + 1e-05)
    span = keep.shape[2]
    for p in range(2 * keep.shape[0]):
        source = pl.ds(pl.multiple_of((client ^ p) * span, span), span)
        target = send if p % 2 else keep
        target[p // 2] = (rows[:, source] * scale * gain[:, source]).astype(bf16)


def select_rows(token_ids, place, norm_gain, embed_table, clients):
    tokens, width = token_ids.shape[0], embed_table.shape[1]
    half = jax.ShapeDtypeStruct((clients // 2, tokens, width // clients), bf16)
    return pl.pallas_call(
        select_kernel,
        out_shape=(half, half),
        in_specs=[scalars, in_hbm, in_hbm, in_hbm],
        out_specs=(whole, whole),
        scratch_shapes=[
            pltpu.SMEM((tokens,), jnp.int32),
            pltpu.VMEM((1, width), f32),
            pltpu.VMEM((tokens, width), f32),
            pltpu.SMEM((tokens + 1,), jnp.int32),
            pltpu.VMEM((fetch_slots, group_rows, width), bf16),
            pltpu.SemaphoreType.DMA((fetch_slots,)),
            pltpu.SemaphoreType.DMA((2,)),
        ],
        compiler_params=vmem_params(48),
        cost_estimate=cost(4e6, 4e6),
        name="select_rows",
    )(place, token_ids, norm_gain[None, :], embed_table)


def standardized(hidden, axis):
    count = hidden.shape[axis]
    center = jnp.sum(hidden, axis=axis, keepdims=True) * (1.0 / count)
    shifted = hidden - center
    spread = jnp.sum(shifted * shifted, axis=axis, keepdims=True) * (1.0 / count)
    return (shifted * lax.rsqrt(spread + 1e-06)).astype(bf16)


def gated(gate, up):
    return gate / (1.0 + jnp.exp(-gate)) * up


def client_kernel(first, place, *refs):
    *blocks, gate_w, up_w, out = refs
    client = place[1]
    tokens, span = blocks[0].shape
    wide = out.shape[1]
    units = pl.ds(pl.multiple_of((first + pl.program_id(0)) * wide, wide), wide)
    gate = jnp.zeros((tokens, wide), f32)
    up = jnp.zeros((tokens, wide), f32)
    for p, block in enumerate(blocks):
        features = pl.ds(pl.multiple_of((client ^ p) * span, span), span)
        gate += jnp.dot(block[...], gate_w[0, features, :], preferred_element_type=f32)
        up += jnp.dot(block[...], up_w[0, features, units], preferred_element_type=f32)
    out[...] = standardized(gated(gate, up), 0)


def client_activations(place, blocks, client_gate, client_up, first, last):
    tokens = blocks[0].shape[0]
    width, units = client_gate.shape[1], last - first
    wide = unit_block(client_gate.shape[2])
    start = first // wide
    return pl.pallas_call(
        functools.partial(client_kernel, start),
        grid=(units // wide,),
        out_shape=jax.ShapeDtypeStruct((tokens, units), bf16),
        in_specs=[scalars]
        + [whole] * len(blocks)
        + [pl.BlockSpec((1, width, wide), lambda i: (0, 0, start + i)), whole],
        out_specs=pl.BlockSpec((tokens, wide), lambda i: (0, i)),
        compiler_params=vmem_params(12),
        cost_estimate=cost(4 * tokens * width * units, 4 * width * units),
        name="client_activations",
    )(place, *blocks, client_gate, client_up)


def unit_block(units, most=256):
    return most if units % most == 0 else most // 2


def partial_kernel(place, rows, gate_w, up_w, keep, send, total):
    wide = unit_block(gate_w.shape[1])
    for which, weights in enumerate((gate_w, up_w)):
        for at in range(0, weights.shape[1], wide):
            total[which, at : at + wide, :] = lax.dot_general(
                weights[:, at : at + wide],
                rows[...],
                (((0,), (1,)), ((), ())),
                preferred_element_type=f32,
            )
    piece = keep.shape[2]
    for p in range(2 * keep.shape[0]):
        source = pl.ds(pl.multiple_of((place[1] ^ p) * piece, 8), piece)
        for which in range(2):
            if p % 2:
                send[p // 2, which] = total[which, source, :].astype(bf16)
            else:
                keep[p // 2, which] = total[which, source, :]


def reference_partials(place, rows, ref_gate, ref_up, clients):
    tokens, span = rows.shape
    units = ref_gate.shape[1]
    shape = (clients // 2, 2, units // clients, tokens)
    return pl.pallas_call(
        partial_kernel,
        out_shape=(jax.ShapeDtypeStruct(shape, f32), jax.ShapeDtypeStruct(shape, bf16)),
        in_specs=[scalars] + [whole] * 3,
        out_specs=(whole, whole),
        scratch_shapes=[pltpu.VMEM((2, units, tokens), f32)],
        compiler_params=vmem_params(16),
        cost_estimate=cost(4 * tokens * span * units, 4 * span * units),
        name="reference_partials",
    )(place, rows, ref_gate, ref_up)


def matched(rows, columns, total):
    tokens = rows.shape[1]
    colsum = jnp.zeros((rows.shape[0], 128), f32)
    for source in columns:
        wide = unit_block(source.shape[1])
        for i in range(0, source.shape[1], wide):
            some = source[:, i : i + wide]
            r = jnp.dot(rows, some, preferred_element_type=f32)
            w = jnp.exp2(r * (sharpness * log2_e / tokens))
            total += lax.dot_general(
                w.astype(bf16), some, (((1,), (1,)), ((), ())), preferred_element_type=f32
            )
            for k in range(0, wide, 128):
                colsum += w[:, k : k + 128]
    return total, jnp.sum(colsum.T, axis=0, keepdims=True)


def match_kernel(sources, refs, *rest):
    columns, rest = rest[:sources], rest[sources:]
    numerator, sums = rest[-2:]
    before = rest[:-2]
    start = before[0][...] if before else jnp.zeros(numerator.shape, f32)
    numerator[...], row = matched(refs[...], columns, start)
    sums[...] = row + before[1][...] if before else row


def match_last_kernel(refs, columns, before, sums_before, keep, send, sums):
    total, row = matched(refs[...], [columns], before[...])
    tokens, lanes = total.shape[1], 128
    row = row + sums_before[...]
    sums[0:1, :] = row
    weighted = total * refs[...].astype(f32)
    weighted = sum(weighted[:, k : k + lanes] for k in range(0, tokens, lanes))
    sums[1:2, :] = jnp.sum(weighted.T, axis=0, keepdims=True) * (1.0 / tokens)
    by_row = jnp.broadcast_to(1.0 / row, (lanes, total.shape[0])).T
    size = keep.shape[2]
    for p in range(2 * keep.shape[0]):
        target = send if p % 2 else keep
        units = slice(p * size, (p + 1) * size)
        for k in range(0, tokens, lanes):
            target[p // 2, 0, :, k : k + lanes] = (total[units, k : k + lanes] * by_row[units]).astype(
                target.dtype
            )


def join_kernel(group, keep, arrived, factor, factor_arrived, *refs):
    pairs, _, size, tokens = keep.shape
    first, *others = refs[-pairs:]
    lanes = 128
    units = 2 * pairs * size
    rows = [
        jnp.broadcast_to(source[:, group * units : (group + 1) * units], (lanes, units)).T
        for source in (factor, factor_arrived)
    ]
    for h in range(pairs):
        ours = slice(2 * h * size, (2 * h + 1) * size)
        theirs = slice((2 * h + 1) * size, (2 * h + 2) * size)
        for k in range(0, tokens, lanes):
            at = slice(k, k + lanes)
            total = keep[h, group, :, at].astype(f32) * rows[0][ours]
            total += arrived[h, group, :, at].astype(f32) * rows[1][theirs]
            if h:
                others[h - 1][:, at] = total.astype(bf16)
            else:
                first[:, at] = total


def joined(group, keep, arrived, factor, factor_arrived, after):
    pairs, _, size, tokens = keep.shape
    piece = jax.ShapeDtypeStruct((size, tokens), bf16)
    return pl.pallas_call(
        functools.partial(join_kernel, group),
        out_shape=(jax.ShapeDtypeStruct((size, tokens), f32), *[piece] * (pairs - 1)),
        in_specs=[whole] * 4 + [anywhere] * len(after),
        out_specs=(whole,) * pairs,
        compiler_params=vmem_params(16),
        cost_estimate=cost(4 * pairs * size * tokens, 6 * pairs * size * tokens),
        name="joined",
    )(keep, arrived, factor, factor_arrived, *after)


def match_cost(rows, tokens, units):
    return cost(4 * rows * units * tokens, 8 * rows * tokens, rows * units)


def match_specs(rows, tokens, groups):
    high = rows // groups
    by_rows = pl.BlockSpec((high, tokens), lambda j: (j, 0))
    return by_rows, *[pl.BlockSpec((n, high), lambda j: (0, j)) for n in (1, 2)]


def unblocked(value):
    return pl.BlockSpec(value.shape, lambda j: (0, 0))


def match(refs, columns, groups, before=()):
    rows, tokens = refs.shape
    units = sum(source.shape[1] for source in columns)
    by_rows, one_row, _ = match_specs(rows, tokens, groups)
    return pl.pallas_call(
        functools.partial(match_kernel, len(columns)),
        grid=(groups,),
        out_shape=(
            jax.ShapeDtypeStruct((rows, tokens), f32),
            jax.ShapeDtypeStruct((1, rows), f32),
        ),
        in_specs=[by_rows]
        + [unblocked(source) for source in columns]
        + [by_rows, one_row][: len(before)],
        out_specs=(by_rows, one_row),
        compiler_params=vmem_params(24),
        cost_estimate=match_cost(rows, tokens, units),
        name="match",
    )(refs, *columns, *before)


def match_last(refs, columns, before, sums, clients, groups):
    rows, tokens = refs.shape
    by_rows, one_row, two_rows = match_specs(rows, tokens, groups)
    shape = (clients // 2, groups, rows // groups // clients, tokens)
    pieces = pl.BlockSpec((shape[0], 1, shape[2], tokens), lambda j: (0, j, 0, 0))
    halves = jax.ShapeDtypeStruct(shape, bf16)
    return pl.pallas_call(
        match_last_kernel,
        grid=(groups,),
        out_shape=(halves, halves, jax.ShapeDtypeStruct((2, rows), f32)),
        in_specs=[by_rows, unblocked(columns), by_rows, one_row],
        out_specs=(pieces, pieces, two_rows),
        compiler_params=vmem_params(24),
        cost_estimate=match_cost(rows, tokens, columns.shape[1]),
        name="match_last",
    )(refs, columns, before, sums)


def tie_kernel(value, *rest):
    rest[-1][...] = value[...]


def tied(value, *others):
    return pl.pallas_call(
        tie_kernel,
        out_shape=jax.ShapeDtypeStruct(value.shape, value.dtype),
        in_specs=[whole] + [anywhere] * len(others),
        out_specs=whole,
        compiler_params=vmem_params(8),
        name="tied",
    )(value, *others)


def place_kernel(place, *refs):
    *pieces, out, wide, sems = refs
    pieces = pieces[: wide.shape[0]]
    size = wide.shape[1]
    copies = []
    for i, piece in enumerate(pieces):
        at = pl.ds(pl.multiple_of((place[1] ^ i) * size, 8), size)
        wide[i] = piece[...].astype(f32)
        copies.append(pltpu.make_async_copy(wide.at[i], out.at[at, :], sems.at[i]))
        copies[-1].start()
    for copy in copies:
        copy.wait()


def placed(place, pieces, units, after):
    size, tokens = pieces[0].shape
    return pl.pallas_call(
        place_kernel,
        out_shape=jax.ShapeDtypeStruct((units, tokens), f32),
        in_specs=[scalars] + [whole] * len(pieces) + [anywhere] * len(after),
        out_specs=anywhere,
        scratch_shapes=[
            pltpu.VMEM((len(pieces), size, tokens), f32),
            pltpu.SemaphoreType.DMA((len(pieces),)),
        ],
        compiler_params=vmem_params(16),
        cost_estimate=cost(1e5, 6 * units * tokens),
        name="placed",
    )(place, *pieces, *after)


def body(clients, parts, token_ids, embed_table, norm_gain, client_gate, client_up, ref_gate, ref_up):
    client = lax.axis_index("client")
    unit = lax.axis_index("unit")
    place = jnp.stack([client * parts + unit, client]).astype(jnp.int32)
    over_clients = functools.partial(xor_permute, axis="client", size=clients)
    over_units = functools.partial(xor_permute, axis="unit", size=parts)

    def gathered(own, after=()):
        blocks = [own] + [None] * (clients - 1)
        far = tied(own, *after) if after else own
        for p in range(2, clients, 2):
            blocks[p] = over_clients(far, mask=p)
        for p in range(0, clients, 2):
            blocks[p + 1] = over_clients(blocks[p], mask=1)
        return blocks

    def summed_pairs(keep, send):
        return keep.astype(f32) + over_clients(send, mask=1).astype(f32)

    def sent(total):
        return [over_clients(total[p // 2].astype(bf16), mask=p) for p in range(2, clients, 2)]

    def summed(total, arrived):
        mine = total[0]
        for other in arrived:
            mine = mine + other.astype(f32)
        return mine

    keep, send = select_rows(token_ids, place, norm_gain, embed_table, clients)
    total = summed_pairs(keep, send)
    half = total.shape[1] // 2
    halves = [total[:, :half], total[:, half:]]
    halves = [(part, sent(part)) for part in halves]
    early, late = halves
    early = summed(*early).astype(bf16)
    met = over_units(early, mask=1)
    late = summed([tied(late[0][0], met)], late[1]).astype(bf16)
    halves = [early + met, late + over_units(late, mask=1)]
    bit = 2
    while bit < parts:
        halves = [part + over_units(part, mask=bit) for part in halves]
        bit *= 2
    own_rows = jnp.concatenate(halves, axis=0)

    ref_keep, ref_send = reference_partials(place, own_rows, ref_gate, ref_up, clients)
    total = summed_pairs(ref_keep, ref_send)
    arrived = sent(total)
    blocks = gathered(own_rows, [total])
    pre = summed(total, arrived)
    ref_piece = standardized(gated(pre[0], pre[1]), 1)
    even = range(0, parts, 2)
    groups, (piece, tokens) = len(even), ref_piece.shape
    ref_pieces = jnp.stack([over_units(ref_piece, mask=k) if k else ref_piece for k in even])
    refs = jnp.stack(gathered(ref_pieces), axis=1).reshape(groups * clients * piece, tokens)

    units = client_gate.shape[2]
    cuts = [0, 3 * units // 7, units]
    own = [
        client_activations(place, blocks, client_gate, client_up, first, last)
        for first, last in zip(cuts, cuts[1:])
    ]
    theirs = [over_units(part, mask=1) for part in own]
    numerator, sums = match(refs, own, groups)
    numerator, sums = match(refs, theirs[:1], groups, (numerator, sums))
    keep, send, sums = match_last(refs, theirs[1], numerator, sums, clients, groups)
    arrived = over_clients(send, mask=1)

    sums = sums.reshape(2, groups, clients * piece)
    all_sums = sums
    for k in even[1:]:
        other = over_units(sums, mask=k)
        all_sums = all_sums + jnp.stack([other[:, g ^ (k // 2)] for g in range(groups)], axis=1)
    colsum, weighted = all_sums[0], all_sums[1]
    factor = (sums[0] * (1.0 / clients) / colsum).reshape(1, groups * clients * piece)
    factor_arrived = over_clients(factor, mask=1)
    reduced = [None] * groups
    after = ()
    for g in reversed(range(groups)):
        first, *others = joined(g, keep, arrived, factor, factor_arrived, after)
        after = others[:1]
        reduced[g] = first
        for p in range(2, clients, 2):
            reduced[g] = reduced[g] + over_clients(others[p // 2 - 1], mask=p).astype(f32)

    score = (weighted[0] / colsum[0]).reshape(clients, piece)
    here = jnp.arange(clients)[:, None] ^ client == jnp.arange(clients)[None, :]
    score = jnp.sum(jnp.where(here[:, :, None], score[None], 0.0), axis=1)
    score = score.reshape(1, clients * piece)

    mine = reduced[0]
    for k in even[1:]:
        mine = mine + over_units(reduced[k // 2].astype(bf16), mask=k).astype(f32)
    pieces = gathered(mine.astype(bf16))
    merged = placed(place, pieces, units, [score])
    return (merged, score)


def solution(mesh):
    in_specs = (
        P(),
        P(("client", "unit"), None),
        P(),
        P("client", None, "unit"),
        P("client", None, "unit"),
        P("client", "unit"),
        P("client", "unit"),
    )
    out_specs = (P("unit", None), P("client", "unit"))
    local = functools.partial(body, mesh.shape["client"], mesh.shape["unit"])
    return jax.shard_map(local, mesh=mesh, in_specs=in_specs, out_specs=out_specs, check_vma=False)
```
